256 devices in a mesh: gz: 64 (over z, x, y_hi), br: 4 (over y_lo, core).
Axes of the slice: x: 4, y: 4 (y_hi: 2, y_lo: 2; y = y_hi * 2 + y_lo), z: 8, core: 2. Of those that a mesh axis runs over, the one named last changes fastest.
Arguments:
- features: bfloat16 [32, 256, 16, 128], P('br', 'gz'), may hold values from -6 to 6
- tap_weights: bfloat16 [4, 3, 3, 3, 128, 256], P('br'), may hold values from -0.109375 to 0.109375
- branch_bias: float32 [4, 256], P('br'), may hold values from -3 to 3
- proj_weights: bfloat16 [4, 256, 256], P('br'), may hold values from -0.1875 to 0.1875
- out_bias: float32 [256], replicated, may hold values from -3 to 3
- cotangent: bfloat16 [32, 256, 16, 256], P('br', 'gz'), may hold values from -0.75 to 0.75
Outputs:
- head_out: bfloat16 [32, 256, 16, 256], P('br', 'gz')
- feature_grad: bfloat16 [32, 256, 16, 128], P('br', 'gz')
- tap_grads: float32 [4, 3, 3, 3, 128, 256], P('br')
- proj_grads: float32 [4, 256, 256], P('br')
The draws below stay inside these ranges and needn't reach their ends.
All inputs are finite; a program needn't handle non-finite values.
Results may differ from the reference program's by a relative error of at most 0.006.
Values may be sent and summed in bfloat16 or wider, within the bound.
No kernel may reach another device: no remote copies, remote signals or barrier semaphores. Data moves between devices by JAX's collectives and lax.ppermute only.
A program may use at most 128 MiB of HBM per device.

```python
import jax
import jax.numpy as jnp
from jax import lax

PLANES = 4
HEIGHT = 16
WIDTH = 32
C = 128
F = 256
BRANCHES = 4
DEPTH = 256


def block_scale(own_key, extent, pieces, low, top_value):
    level = 1.0
    for position, shards_of in pieces:
        heights = jax.random.uniform(jax.random.fold_in(jax.random.fold_in(own_key, 6), position), (shards_of,), jnp.float32, low / len(pieces), top_value / len(pieces))
        level = level * jnp.repeat(jnp.exp(heights), extent[position] // shards_of).reshape((-1,) + (1,) * (len(extent) - 1 - position))
    return level


def bell_draw(rng, shape, scale, most, shards=(), kind=jnp.bfloat16):
    array = scale * jax.random.normal(rng, shape, jnp.float32)
    if shards:
        array = array * block_scale(rng, shape, shards, -0.22, 0.18)
    return jnp.clip(array, -most, most).astype(kind)


def setup_inputs(seed: int = 0) -> dict:
    streams_of = jax.random.split(jax.random.key(seed), 7)
    features = bell_draw(streams_of[0], (WIDTH, DEPTH, HEIGHT, C), 1.0, 6.0, ((0, 4), (1, 64)))
    tap_weights = bell_draw(streams_of[1], (BRANCHES, 3, 3, 3, C, F), (27 * C) ** -0.5, 0.109375, ((0, 4),))
    branch_bias = bell_draw(streams_of[2], (BRANCHES, F), 0.5, 3.0, ((0, 4),), jnp.float32)
    proj_weights = bell_draw(streams_of[3], (BRANCHES, F, F), (BRANCHES * F) ** -0.5, 0.1875, ((0, 4),))
    out_bias = bell_draw(streams_of[4], (F,), 0.5, 3.0, (), jnp.float32)
    cotangent = bell_draw(streams_of[5], (WIDTH, DEPTH, HEIGHT, F), ((WIDTH * HEIGHT * DEPTH) ** -0.25), 0.75, ((0, 4), (1, 64)))
    return dict(features=features, tap_weights=tap_weights, branch_bias=branch_bias, proj_weights=proj_weights, out_bias=out_bias, cotangent=cotangent)


def silu_slope(values):
    logistic = jax.nn.sigmoid(values)
    return logistic * (1.0 + values * (1.0 - logistic))


def tap_mask(branch):
    depth_pos = jnp.arange(3)[:, None, None]
    row_pos = jnp.arange(3)[None, :, None]
    col_pos = jnp.arange(3)[None, None, :]
    centre = (depth_pos == 1) & (row_pos == 1) & (col_pos == 1)
    return jnp.where((branch > 0) | centre, 1.0, 0.0).astype(jnp.float32)


def in_plane(values):
    breadth = values.shape[0]
    height = values.shape[2]
    padded = jnp.pad(values, ((1, 1), (0, 0), (1, 1), (0, 0)))
    return jnp.concatenate([padded[across:across + breadth, :, upward:upward + height, :] for across in range(3) for upward in range(3)], axis=-1)


def depth_shift(values, offset):
    reach_max = 4 * PLANES
    planes_all = values.shape[1]
    padded = jnp.pad(values, ((0, 0), (reach_max, reach_max), (0, 0), (0, 0)))
    return padded[:, reach_max + offset:reach_max + offset + planes_all]


def reference(features, tap_weights, branch_bias, proj_weights, out_bias, cotangent):
    channels = features.shape[3]
    hidden_width = tap_weights.shape[5]
    columns = in_plane(features)
    summed = jnp.zeros(features.shape[:3] + (hidden_width,), jnp.float32) + out_bias.astype(jnp.float32)
    preact_list = []
    hidden_list = []
    masked_list = []
    for branch in range(BRANCHES):
        dilation = PLANES * 2 ** (branch - 1) if branch > 0 else 0
        masked = tap_weights[branch] * tap_mask(branch).astype(jnp.bfloat16)[:, :, :, None, None]
        preact = jnp.zeros(summed.shape, jnp.float32) + branch_bias[branch].astype(jnp.float32)
        for tap_index in range(3):
            preact = preact + jnp.dot(depth_shift(columns, (tap_index - 1) * dilation), masked[tap_index].reshape(9 * channels, hidden_width), preferred_element_type=jnp.float32)
        hidden = jax.nn.silu(preact).astype(jnp.bfloat16)
        summed = summed + jnp.dot(hidden, proj_weights[branch], preferred_element_type=jnp.float32)
        preact_list.append(preact)
        hidden_list.append(hidden)
        masked_list.append(masked)
    head_out = jax.nn.silu(summed).astype(jnp.bfloat16)
    d_out = (cotangent.astype(jnp.float32) * silu_slope(summed)).astype(jnp.bfloat16)
    flat_out = d_out.reshape(-1, hidden_width)
    feature_grad = jnp.zeros(features.shape, jnp.float32)
    tap_list = []
    proj_list = []
    for branch in range(BRANCHES):
        dilation = PLANES * 2 ** (branch - 1) if branch > 0 else 0
        masked = masked_list[branch]
        flat_hidden = hidden_list[branch].reshape(-1, hidden_width)
        proj_list.append(lax.dot_general(flat_hidden, flat_out, (((0,), (0,)), ((), ())), preferred_element_type=jnp.float32))
        d_hidden = lax.dot_general(d_out, proj_weights[branch], (((3,), (1,)), ((), ())), preferred_element_type=jnp.float32)
        d_pre = (d_hidden * silu_slope(preact_list[branch])).astype(jnp.bfloat16)
        flat_pre = d_pre.reshape(-1, hidden_width)
        per_tap = [lax.dot_general(depth_shift(columns, (tap_index - 1) * dilation).reshape(-1, 9 * channels), flat_pre, (((0,), (0,)), ((), ())), preferred_element_type=jnp.float32) for tap_index in range(3)]
        tap_list.append(jnp.stack(per_tap).reshape(3, 3, 3, channels, hidden_width) * tap_mask(branch)[:, :, :, None, None])
        flipped = masked[:, ::-1, ::-1].transpose(0, 1, 2, 4, 3).reshape(3, 9 * hidden_width, channels)
        d_columns = in_plane(d_pre)
        for tap_index in range(3):
            feature_grad = feature_grad + depth_shift(jnp.dot(d_columns, flipped[tap_index], preferred_element_type=jnp.float32), -(tap_index - 1) * dilation)
    return head_out, feature_grad.astype(jnp.bfloat16), jnp.stack(tap_list), jnp.stack(proj_list)
```

```python
import functools

import jax
import jax.numpy as jnp
from jax import lax
from jax.experimental import pallas as pl
from jax.experimental.pallas import tpu as pltpu
from jax.sharding import Mesh
from jax.sharding import PartitionSpec as P

C = 128
F = 256
COL = 64
ROWS = 2048
QUART = 512
TAPS = 27 * C
GRAD_ROWS = TAPS + F
bf16 = jnp.bfloat16
f32 = jnp.float32
GZ = ("z", "x", "yh")
BR = ("yl", "c")
SWAP = [(0, 1), (1, 0)]
VMEM = pl.BlockSpec(memory_space=pltpu.VMEM)
SMEM = pl.BlockSpec(memory_space=pltpu.SMEM)


def silu_slope(values):
    logistic = jax.nn.sigmoid(values)
    return logistic * (1.0 + values * (1.0 - logistic))


def height_of(rows, lanes):
    return lax.broadcasted_iota(jnp.int32, (rows, lanes), 0) & 15


def from_below(values):
    rolled = pltpu.roll(values, 1, 0)
    return jnp.where(height_of(*values.shape) == 0, 0.0, rolled)


def from_above(values):
    rolled = pltpu.roll(values, values.shape[0] - 1, 0)
    return jnp.where(height_of(*values.shape) == 15, 0.0, rolled)


def matmul(lhs, rhs):
    return jnp.dot(lhs, rhs, preferred_element_type=f32)


def matmul_rt(lhs, rhs):
    return lax.dot_general(lhs, rhs, (((1,), (1,)), ((), ())), preferred_element_type=f32)


def forward_kernel(core_ref, below, centre, above, weights, bias, proj, preact, hidden, keep, send, padded):
    for t, slab in enumerate((below, centre, above)):
        padded[t, 0:COL] = jnp.zeros((COL, C), bf16)
        padded[t, COL + ROWS : 2 * COL + ROWS] = jnp.zeros((COL, C), bf16)
        padded[t, COL : COL + ROWS] = slab[...]
    core = core_ref[0]
    for q in range(4):
        start = q * QUART
        window = jnp.concatenate(
            [padded[t, start + i * COL : start + i * COL + QUART] for t in range(3) for i in range(3)], axis=1
        )
        parts = matmul(window, weights[...])
        value = bias[...] + parts[:, F : 2 * F]
        value = value + from_below(parts[:, :F]) + from_above(parts[:, 2 * F :])
        preact[start : start + QUART] = value
        active = (value * jax.nn.sigmoid(value)).astype(bf16)
        hidden[start : start + QUART] = active
        projected = matmul(active, proj[...])

        @pl.when(core == q % 2)
        def _():
            keep[q // 2] = projected

        @pl.when(core != q % 2)
        def _():
            send[q // 2] = projected.astype(bf16)


def prepare_kernel(below, centre, above, preact, hidden, slope, hidden_t, features_t):
    for q in range(4):
        cells = slice(q * QUART, (q + 1) * QUART)
        slope[cells] = silu_slope(preact[cells])
        hidden_t[:, cells] = hidden[cells].astype(f32).T.astype(bf16)
        for t, slab in enumerate((below, centre, above)):
            value = slab[cells].astype(f32)
            for j, moved in enumerate((from_below(value), value, from_above(value))):
                block = (t * 3 + j) * C
                features_t[block : block + C, cells] = moved.T.astype(bf16)


def feature_kernel(core_ref, own, other, slope, proj, weights, d_pre, low, mid, high):
    d_pre[0:COL] = jnp.zeros((COL, F), bf16)
    d_pre[COL + ROWS : 2 * COL + ROWS] = jnp.zeros((COL, F), bf16)
    for q in range(4):
        start = q * QUART
        mine = core_ref[0] == q % 2
        rows = jnp.where(mine, own[q // 2], other[q // 2])
        d_hidden = matmul_rt(rows, proj[...])
        d_pre[COL + start : COL + start + QUART] = (d_hidden * slope[start : start + QUART]).astype(bf16)
    for q in range(4):
        start = q * QUART
        window = jnp.concatenate(
            [d_pre[start + (2 - i) * COL : start + (2 - i) * COL + QUART] for i in range(3)], axis=1
        )
        parts = matmul_rt(window, weights[...])
        total = parts[:, 3 * C : 6 * C] + from_above(parts[:, : 3 * C]) + from_below(parts[:, 6 * C :])
        cells = slice(start, start + QUART)
        low[cells] = total[:, :C].astype(bf16)
        mid[cells] = total[:, C : 2 * C]
        high[cells] = total[:, 2 * C :].astype(bf16)


def gradient_kernel(core_ref, keep_ref, d_pre, features_t, hidden_t, own, other, grads, window, d_out):
    for i in range(3):
        window[:, i * F : (i + 1) * F] = d_pre[(2 - i) * COL : (2 - i) * COL + ROWS]
    off_centre = keep_ref[0]
    for t in range(3):
        block = matmul(features_t[t * 3 * C : (t + 1) * 3 * C], window[...])
        for i in range(3):
            for j in range(3):
                tap = (t * 9 + i * 3 + j) * C
                piece = block[j * C : (j + 1) * C, i * F : (i + 1) * F]
                if (t, i, j) != (1, 1, 1):
                    piece = piece * off_centre
                grads[tap : tap + C] = piece.astype(bf16)
    for q in range(4):
        mine = core_ref[0] == q % 2
        d_out[q * QUART : (q + 1) * QUART] = jnp.where(mine, own[q // 2], other[q // 2])
    grads[TAPS:] = matmul(hidden_t[...], d_out[...]).astype(bf16)


def call(kernel, outs, specs, scratch, flops, *args):
    return pl.pallas_call(
        kernel,
        out_shape=[jax.ShapeDtypeStruct(*o) for o in outs],
        in_specs=specs,
        out_specs=[VMEM] * len(outs),
        scratch_shapes=scratch,
        compiler_params=pltpu.CompilerParams(vmem_limit_bytes=44 * 1024 * 1024),
        cost_estimate=pl.CostEstimate(flops=flops, bytes_accessed=8_000_000, transcendentals=0),
    )(*args)


def depth_pairs(mesh_gz, sign):
    strides = (0, 1, 2, 4)
    pairs = []
    for g in range(mesh_gz):
        for b in range(1, 4):
            target = g + sign * strides[b]
            if 0 <= target < mesh_gz:
                pairs.append((g * 4 + b, target * 4 + b))
    return pairs


def gathered(values, axis, peers):
    return lax.all_to_all(jnp.broadcast_to(values[None], (peers,) + values.shape), axis, 0, 0, tiled=True)


def shards(slabs, features, tap_weights, branch_bias, proj_weights, out_bias, cotangent):
    branch = lax.axis_index(BR)
    core = lax.axis_index("c")
    core_arg = core.astype(jnp.int32)[None]
    up = depth_pairs(slabs, 1)
    down = depth_pairs(slabs, -1)
    everywhere = GZ + BR
    proj = proj_weights[0]

    centre = lax.all_gather(features.reshape(QUART, C), BR, axis=0, tiled=True)
    below = lax.ppermute(centre, everywhere, up)
    above = lax.ppermute(centre, everywhere, down)

    tap = jnp.arange(27).reshape(3, 3, 3)
    off_centre = jnp.where(branch > 0, 1.0, 0.0).astype(f32)
    mask = jnp.where(tap == 13, 1.0, off_centre).astype(bf16)
    masked = tap_weights[0] * mask[:, :, :, None, None]
    weights_fwd = masked.transpose(0, 1, 3, 2, 4).reshape(9 * C, 3 * F)
    weights_bwd = masked.transpose(2, 0, 3, 1, 4).reshape(9 * C, 3 * F)
    cot_mine = cotangent.reshape(QUART, F)
    cot_pair = lax.ppermute(cot_mine, "yl", SWAP)

    preact, hidden, keep, send = call(
        forward_kernel,
        [((ROWS, F), f32), ((ROWS, F), bf16), ((2, QUART, F), f32), ((2, QUART, F), bf16)],
        [SMEM] + [VMEM] * 6,
        [pltpu.VMEM((3, ROWS + 2 * COL, C), bf16)],
        2 * ROWS * 27 * C * F,
        core_arg, below, centre, above, weights_fwd, branch_bias, proj,
    )
    chip_sum = keep + lax.ppermute(send, "c", SWAP).astype(f32)
    slope, hidden_t, features_t = call(
        prepare_kernel,
        [((ROWS, F), f32), ((F, ROWS), bf16), ((9 * C, ROWS), bf16)],
        [VMEM] * 5,
        [],
        2 * ROWS * 9 * C * F,
        below, centre, above, preact, hidden,
    )
    summed = chip_sum + lax.ppermute(chip_sum.astype(bf16), "yl", SWAP).astype(f32) + out_bias
    row = lax.axis_index("yl")
    first = row == 0
    cot = jnp.stack([jnp.where(first, cot_mine, cot_pair), jnp.where(first, cot_pair, cot_mine)])
    own = (cot.astype(f32) * silu_slope(summed)).astype(bf16)
    head_out = jax.nn.silu(jnp.where(first, summed[0], summed[1])).astype(bf16)
    other = lax.ppermute(own, "c", SWAP)

    d_pre, low, mid, high = call(
        feature_kernel,
        [((ROWS + 2 * COL, F), bf16), ((ROWS, C), bf16), ((ROWS, C), f32), ((ROWS, C), bf16)],
        [SMEM] + [VMEM] * 5,
        [],
        2 * ROWS * 27 * C * F,
        core_arg, own, other, slope, proj, weights_bwd,
    )
    from_low = lax.ppermute(low, everywhere, down)
    from_high = lax.ppermute(high, everywhere, up)
    (grads,) = call(
        gradient_kernel,
        [((GRAD_ROWS, F), bf16)],
        [SMEM, SMEM] + [VMEM] * 5,
        [pltpu.VMEM((ROWS, 3 * F), bf16), pltpu.VMEM((ROWS, F), bf16)],
        2 * ROWS * 27 * C * F,
        core_arg, off_centre[None], d_pre, features_t, hidden_t, own, other,
    )

    plane = lax.axis_size("x") * lax.axis_size("yh")
    tall = lax.axis_size("z")
    part = lax.all_to_all(grads.reshape(plane, GRAD_ROWS // plane, F), ("x", "yh"), 0, 0, tiled=True)
    part = jnp.sum(part.astype(f32), axis=0).astype(bf16)
    part = lax.all_to_all(part.reshape(tall, GRAD_ROWS // plane // tall, F), "z", 0, 0, tiled=True)
    part = jnp.sum(part.astype(f32), axis=0).astype(bf16)
    part = gathered(part, "z", tall).reshape(GRAD_ROWS // plane, F)
    total = gathered(part, ("x", "yh"), plane).reshape(GRAD_ROWS, F).astype(f32)

    branch_grad = (mid + from_low.astype(f32) + from_high.astype(f32)).reshape(2, 2, QUART, C)
    sent = lax.dynamic_index_in_dim(branch_grad, 1 - core, 1, keepdims=False).astype(bf16)
    kept = lax.dynamic_index_in_dim(branch_grad, core, 1, keepdims=False)
    chip_grad = kept + lax.ppermute(sent, "c", SWAP).astype(f32)
    sent = lax.dynamic_index_in_dim(chip_grad, 1 - row, 0, keepdims=False).astype(bf16)
    kept = lax.dynamic_index_in_dim(chip_grad, row, 0, keepdims=False)
    feature_grad = (kept + lax.ppermute(sent, "yl", SWAP).astype(f32)).astype(bf16)

    return (
        head_out.reshape(cotangent.shape),
        feature_grad.reshape(features.shape),
        total[:TAPS].reshape(1, 3, 3, 3, C, F),
        total[TAPS:].reshape(1, F, F),
    )


def solution(mesh):
    slabs = mesh.shape["gz"]
    split = (8, 4, 2) if slabs == 64 else (slabs, 1, 1)
    fine = Mesh(mesh.devices.reshape(split + (2, 2)), GZ + BR)
    in_specs = (
        P(BR, GZ, None, None),
        P(BR, None, None, None, None, None),
        P(BR, None),
        P(BR, None, None),
        P(),
        P(BR, GZ, None, None),
    )
    out_specs = (
        P(BR, GZ, None, None),
        P(BR, GZ, None, None),
        P(BR, None, None, None, None, None),
        P(BR, None, None),
    )
    return jax.shard_map(
        functools.partial(shards, slabs), mesh=fine, in_specs=in_specs, out_specs=out_specs, check_vma=False
    )
```

```python
import functools

import jax
import jax.numpy as jnp
from jax import lax
from jax.experimental import pallas as pl
from jax.experimental.pallas import tpu as pltpu
from jax.sharding import Mesh
from jax.sharding import PartitionSpec as P

C = 128
F = 256
COL = 64
ROWS = 2048
QUART = 512
TAPS = 27 * C
GRAD_ROWS = TAPS + F
bf16 = jnp.bfloat16
f32 = jnp.float32
GZ = ("z", "x", "yh")
BR = ("yl", "c")
SWAP = [(0, 1), (1, 0)]
VMEM = pl.BlockSpec(memory_space=pltpu.VMEM)
SMEM = pl.BlockSpec(memory_space=pltpu.SMEM)


def silu_slope(values):
    logistic = jax.nn.sigmoid(values)
    return logistic * (1.0 + values * (1.0 - logistic))


def height_of(rows, lanes):
    return lax.broadcasted_iota(jnp.int32, (rows, lanes), 0) & 15


def from_below(values):
    rolled = pltpu.roll(values, 1, 0)
    return jnp.where(height_of(*values.shape) == 0, 0.0, rolled)


def from_above(values):
    rolled = pltpu.roll(values, values.shape[0] - 1, 0)
    return jnp.where(height_of(*values.shape) == 15, 0.0, rolled)


def matmul(lhs, rhs):
    return jnp.dot(lhs, rhs, preferred_element_type=f32)


def matmul_rt(lhs, rhs):
    return lax.dot_general(lhs, rhs, (((1,), (1,)), ((), ())), preferred_element_type=f32)


def pad_columns(padded, slab):
    padded[0:COL] = jnp.zeros((COL, C), bf16)
    padded[COL + ROWS : 2 * COL + ROWS] = jnp.zeros((COL, C), bf16)
    padded[COL : COL + ROWS] = slab[...]


def over_height(parts):
    return parts[:, F : 2 * F] + from_below(parts[:, :F]) + from_above(parts[:, 2 * F :])


def centre_kernel(centre, weights, bias, base, padded):
    pad_columns(padded, centre)
    for q in range(4):
        start = q * QUART
        window = jnp.concatenate([padded[start + i * COL : start + i * COL + QUART] for i in range(3)], axis=1)
        base[start : start + QUART] = bias[...] + over_height(matmul(window, weights[3 * C : 6 * C]))


def forward_kernel(core_ref, below, above, weights, base, proj, preact, hidden, keep, send, low, high, outer):
    pad_columns(low, below)
    pad_columns(high, above)
    outer[: 3 * C] = weights[: 3 * C]
    outer[3 * C :] = weights[6 * C :]
    core = core_ref[0]
    for q in range(4):
        start = q * QUART
        window = jnp.concatenate(
            [slab[start + i * COL : start + i * COL + QUART] for slab in (low, high) for i in range(3)], axis=1
        )
        value = base[start : start + QUART] + over_height(matmul(window, outer[...]))
        preact[start : start + QUART] = value
        active = (value * jax.nn.sigmoid(value)).astype(bf16)
        hidden[start : start + QUART] = active
        projected = matmul(active, proj[...])

        @pl.when(core == q % 2)
        def _():
            keep[q // 2] = projected

        @pl.when(core != q % 2)
        def _():
            send[q // 2] = projected.astype(bf16)


def prepare_kernel(below, centre, above, preact, hidden, slope, hidden_t, features_t):
    for q in range(4):
        cells = slice(q * QUART, (q + 1) * QUART)
        slope[cells] = silu_slope(preact[cells])
        hidden_t[:, cells] = hidden[cells].astype(f32).T.astype(bf16)
        for t, slab in enumerate((below, centre, above)):
            value = slab[cells].astype(f32)
            for j, moved in enumerate((from_below(value), value, from_above(value))):
                block = (t * 3 + j) * C
                features_t[block : block + C, cells] = moved.T.astype(bf16)


def output_kernel(row_ref, chip_sum, recv, bias, cot_mine, cot_pair, own, head_out):
    row = row_ref[0]
    mine = chip_sum[row] + recv[row].astype(f32) + bias[...]
    head_out[...] = (mine * jax.nn.sigmoid(mine)).astype(bf16)
    own[row] = (cot_mine[...].astype(f32) * silu_slope(mine)).astype(bf16)
    pair = chip_sum[1 - row] + recv[1 - row].astype(f32) + bias[...]
    own[1 - row] = (cot_pair[...].astype(f32) * silu_slope(pair)).astype(bf16)


def gradient_kernel(
    core_ref, keep_ref, own, other, slope, proj, features_t, hidden_t, grads, d_pre, window, d_out
):
    d_pre[0:COL] = jnp.zeros((COL, F), bf16)
    d_pre[COL + ROWS : 2 * COL + ROWS] = jnp.zeros((COL, F), bf16)
    for q in range(4):
        start = q * QUART
        rows = jnp.where(core_ref[0] == q % 2, own[q // 2], other[q // 2])
        d_out[start : start + QUART] = rows
        d_hidden = matmul_rt(rows, proj[...])
        d_pre[COL + start : COL + start + QUART] = (d_hidden * slope[start : start + QUART]).astype(bf16)
    for i in range(3):
        window[:, i * F : (i + 1) * F] = d_pre[(2 - i) * COL : (2 - i) * COL + ROWS]
    off_centre = keep_ref[0]
    for t in range(3):
        block = matmul(features_t[t * 3 * C : (t + 1) * 3 * C], window[...])
        for i in range(3):
            for j in range(3):
                tap = (t * 9 + i * 3 + j) * C
                piece = block[j * C : (j + 1) * C, i * F : (i + 1) * F]
                if (t, i, j) != (1, 1, 1):
                    piece = piece * off_centre
                grads[tap : tap + C] = piece.astype(bf16)
    grads[TAPS:] = matmul(hidden_t[...], d_out[...]).astype(bf16)


def feature_kernel(d_pre, weights, low, mid, high):
    for q in range(4):
        start = q * QUART
        window = jnp.concatenate(
            [d_pre[start + (2 - i) * COL : start + (2 - i) * COL + QUART] for i in range(3)], axis=1
        )
        parts = matmul_rt(window, weights[...])
        total = parts[:, 3 * C : 6 * C] + from_above(parts[:, : 3 * C]) + from_below(parts[:, 6 * C :])
        cells = slice(start, start + QUART)
        low[cells] = total[:, :C].astype(bf16)
        mid[cells] = total[:, C : 2 * C]
        high[cells] = total[:, 2 * C :].astype(bf16)


def first_sum_kernel(parts, total):
    rows = parts.shape[1]
    acc = parts[0].astype(f32)
    for k in range(1, parts.shape[0]):
        acc = acc + parts[k].astype(f32)
    total[0:rows] = acc.astype(bf16)
    if total.shape[0] > rows:
        total[rows:] = jnp.zeros((total.shape[0] - rows, F), bf16)


def second_sum_kernel(parts, copies):
    acc = parts[0].astype(f32)
    for k in range(1, parts.shape[0]):
        acc = acc + parts[k].astype(f32)
    total = acc.astype(bf16)
    for k in range(copies.shape[0]):
        copies[k] = total


def call(kernel, outs, specs, scratch, flops, *args):
    return pl.pallas_call(
        kernel,
        out_shape=[jax.ShapeDtypeStruct(*o) for o in outs],
        in_specs=specs,
        out_specs=[VMEM] * len(outs),
        scratch_shapes=scratch,
        compiler_params=pltpu.CompilerParams(vmem_limit_bytes=16 * 1024 * 1024),
        cost_estimate=pl.CostEstimate(flops=flops, bytes_accessed=8_000_000, transcendentals=0),
    )(*args)


def depth_pairs(mesh_gz, sign):
    strides = (0, 1, 2, 4)
    pairs = []
    for g in range(mesh_gz):
        for b in range(1, 4):
            target = g + sign * strides[b]
            if 0 <= target < mesh_gz:
                pairs.append((g * 4 + b, target * 4 + b))
    return pairs


def shards(slabs, features, tap_weights, branch_bias, proj_weights, out_bias, cotangent):
    branch = lax.axis_index(BR)
    core = lax.axis_index("c")
    row = lax.axis_index("yl")
    core_arg = core.astype(jnp.int32)[None]
    row_arg = row.astype(jnp.int32)[None]
    up = depth_pairs(slabs, 1)
    down = depth_pairs(slabs, -1)
    everywhere = GZ + BR
    proj = proj_weights[0]

    centre = lax.all_gather(features.reshape(QUART, C), BR, axis=0, tiled=True)
    tap = jnp.arange(27).reshape(3, 3, 3)
    off_centre = jnp.where(branch > 0, 1.0, 0.0).astype(f32)
    mask = jnp.where(tap == 13, 1.0, off_centre).astype(bf16)
    cot_mine = cotangent.reshape(QUART, F)
    centre, cot_mine = lax.optimization_barrier((centre, cot_mine))
    below = lax.ppermute(centre, everywhere, up)
    above = lax.ppermute(centre, everywhere, down)
    cot_pair = lax.ppermute(cot_mine, "yl", SWAP)
    masked = tap_weights[0] * mask[:, :, :, None, None]
    weights_fwd = masked.transpose(0, 1, 3, 2, 4).reshape(9 * C, 3 * F)
    weights_bwd = masked.transpose(2, 0, 3, 1, 4).reshape(9 * C, 3 * F)
    (base,) = call(
        centre_kernel,
        [((ROWS, F), f32)],
        [VMEM] * 3,
        [pltpu.VMEM((ROWS + 2 * COL, C), bf16)],
        2 * ROWS * 9 * C * F,
        centre, weights_fwd, branch_bias,
    )
    below, above, cot_pair, base, weights_bwd = lax.optimization_barrier((below, above, cot_pair, base, weights_bwd))

    preact, hidden, keep, send = call(
        forward_kernel,
        [((ROWS, F), f32), ((ROWS, F), bf16), ((2, QUART, F), f32), ((2, QUART, F), bf16)],
        [SMEM] + [VMEM] * 5,
        [pltpu.VMEM((ROWS + 2 * COL, C), bf16)] * 2 + [pltpu.VMEM((6 * C, 3 * F), bf16)],
        2 * ROWS * 18 * C * F,
        core_arg, below, above, weights_fwd, base, proj,
    )
    chip_sum = keep + lax.ppermute(send, "c", SWAP).astype(f32)
    chip_send, preact, hidden = lax.optimization_barrier((chip_sum.astype(bf16), preact, hidden))
    recv = lax.ppermute(chip_send, "yl", SWAP)
    slope, hidden_t, features_t = call(
        prepare_kernel,
        [((ROWS, F), f32), ((F, ROWS), bf16), ((9 * C, ROWS), bf16)],
        [VMEM] * 5,
        [],
        2 * ROWS * 9 * C * F,
        below, centre, above, preact, hidden,
    )
    recv, slope, hidden_t, features_t = lax.optimization_barrier((recv, slope, hidden_t, features_t))
    own, head_out = call(
        output_kernel,
        [((2, QUART, F), bf16), ((QUART, F), bf16)],
        [SMEM] + [VMEM] * 5,
        [],
        1_000_000,
        row_arg, chip_sum, recv, out_bias[None], cot_mine, cot_pair,
    )
    other = lax.ppermute(own, "c", SWAP)

    grads, d_pre = call(
        gradient_kernel,
        [((GRAD_ROWS, F), bf16), ((ROWS + 2 * COL, F), bf16)],
        [SMEM, SMEM] + [VMEM] * 6,
        [pltpu.VMEM((ROWS, 3 * F), bf16), pltpu.VMEM((ROWS, F), bf16)],
        2 * ROWS * 27 * C * F,
        core_arg, off_centre[None], own, other, slope, proj, features_t, hidden_t,
    )
    plane = lax.axis_size("x") * lax.axis_size("yh")
    tall = lax.axis_size("z")
    share = GRAD_ROWS // plane
    piece = -(-share // (16 * tall)) * 16
    part = lax.all_to_all(grads.reshape(plane, share, F), ("x", "yh"), 0, 0, tiled=True)
    low, mid, high = call(
        feature_kernel,
        [((ROWS, C), bf16), ((ROWS, C), f32), ((ROWS, C), bf16)],
        [VMEM] * 2,
        [],
        2 * ROWS * 27 * C * F,
        d_pre, weights_bwd,
    )
    part, low, mid, high = lax.optimization_barrier((part, low, mid, high))
    from_low = lax.ppermute(low, everywhere, down)
    from_high = lax.ppermute(high, everywhere, up)
    (part,) = call(first_sum_kernel, [((tall * piece, F), bf16)], [VMEM], [], 1_000_000, part)
    part = lax.all_to_all(part.reshape(tall, piece, F), "z", 0, 0, tiled=True)
    (part,) = call(second_sum_kernel, [((tall, piece, F), bf16)], [VMEM], [], 100_000, part)
    part, from_low, from_high = lax.optimization_barrier((part, from_low, from_high))
    part = lax.all_to_all(part, "z", 0, 0, tiled=True).reshape(tall * piece, F)

    branch_grad = (mid + from_low.astype(f32) + from_high.astype(f32)).reshape(2, 2, QUART, C)
    sent = lax.dynamic_index_in_dim(branch_grad, 1 - core, 1, keepdims=False).astype(bf16)
    kept = lax.dynamic_index_in_dim(branch_grad, core, 1, keepdims=False)
    chip_grad = kept + lax.ppermute(sent, "c", SWAP).astype(f32)
    sent = lax.dynamic_index_in_dim(chip_grad, 1 - row, 0, keepdims=False).astype(bf16)
    kept = lax.dynamic_index_in_dim(chip_grad, row, 0, keepdims=False)
    feature_grad = (kept + lax.ppermute(sent, "yl", SWAP).astype(f32)).astype(bf16)
    part, feature_grad = lax.optimization_barrier((part, feature_grad))

    copies = jnp.broadcast_to(part[None, :share], (plane, share, F))
    total = lax.all_to_all(copies, ("x", "yh"), 0, 0, tiled=True).reshape(GRAD_ROWS, F)
    tap_total = total[:TAPS].astype(f32)
    proj_total = total[TAPS:].astype(f32)

    return (
        head_out.reshape(cotangent.shape),
        feature_grad.reshape(features.shape),
        tap_total.reshape(1, 3, 3, 3, C, F),
        proj_total.reshape(1, F, F),
    )


def solution(mesh):
    slabs = mesh.shape["gz"]
    split = (8, 4, 2) if slabs == 64 else (slabs, 1, 1)
    fine = Mesh(mesh.devices.reshape(split + (2, 2)), GZ + BR)
    in_specs = (
        P(BR, GZ, None, None),
        P(BR, None, None, None, None, None),
        P(BR, None),
        P(BR, None, None),
        P(),
        P(BR, GZ, None, None),
    )
    out_specs = (
        P(BR, GZ, None, None),
        P(BR, GZ, None, None),
        P(BR, None, None, None, None, None),
        P(BR, None, None),
    )
    return jax.shard_map(
        functools.partial(shards, slabs), mesh=fine, in_specs=in_specs, out_specs=out_specs, check_vma=False
    )
```

```python
import functools

import jax
import jax.numpy as jnp
from jax import lax
from jax.experimental import pallas as pl
from jax.experimental.pallas import tpu as pltpu
from jax.sharding import Mesh
from jax.sharding import PartitionSpec as P

C = 128
F = 256
COL = 64
ROWS = 2048
HALF = 1024
QUART = 512
TAPS = 27 * C
GRAD_ROWS = TAPS + F
bf16 = jnp.bfloat16
f32 = jnp.float32
GZ = ("zh", "zl", "x", "yh")
NEAR = ("zl", "x", "yh")
BR = ("yl", "c")
SWAP = [(0, 1), (1, 0)]
VMEM = pl.BlockSpec(memory_space=pltpu.VMEM)
HBM = pl.BlockSpec(memory_space=pltpu.HBM)
SMEM = pl.BlockSpec(memory_space=pltpu.SMEM)


def silu_slope(values):
    logistic = jax.nn.sigmoid(values)
    return logistic * (1.0 + values * (1.0 - logistic))


def height_of(rows, lanes):
    return lax.broadcasted_iota(jnp.int32, (rows, lanes), 0) & 15


def from_below(values):
    rolled = pltpu.roll(values, 1, 0)
    return jnp.where(height_of(*values.shape) == 0, 0.0, rolled)


def from_above(values):
    rolled = pltpu.roll(values, values.shape[0] - 1, 0)
    return jnp.where(height_of(*values.shape) == 15, 0.0, rolled)


def matmul(lhs, rhs):
    return jnp.dot(lhs, rhs, preferred_element_type=f32)


def matmul_rt(lhs, rhs):
    return lax.dot_general(lhs, rhs, (((1,), (1,)), ((), ())), preferred_element_type=f32)


def pad_columns(padded, slab):
    padded[0:COL] = jnp.zeros((COL, C), bf16)
    padded[COL + ROWS : 2 * COL + ROWS] = jnp.zeros((COL, C), bf16)
    padded[COL : COL + ROWS] = slab[...]


def pad_half(padded, slab, half):
    if half == 0:
        padded[0:COL] = jnp.zeros((COL, C), bf16)
        padded[COL:] = slab[0 : HALF + COL]
    else:
        padded[0 : HALF + COL] = slab[HALF - COL :]
        padded[HALF + COL :] = jnp.zeros((COL, C), bf16)


def over_height(parts):
    return parts[:, F : 2 * F] + from_below(parts[:, :F]) + from_above(parts[:, 2 * F :])


def centre_kernel(centre, weights, bias, base, padded):
    pad_columns(padded, centre)
    for q in range(4):
        start = q * QUART
        window = jnp.concatenate([padded[start + i * COL : start + i * COL + QUART] for i in range(3)], axis=1)
        base[start : start + QUART] = bias[...] + over_height(matmul(window, weights[...]))


def forward_kernel(half, core_ref, below, above, weights, base, proj, preact, hidden, keep, send, low, high):
    pad_half(low, below, half)
    pad_half(high, above, half)
    core = core_ref[0]
    for side in range(2):
        start = side * QUART
        cells = slice(start, start + QUART)
        window = jnp.concatenate(
            [slab[start + i * COL : start + i * COL + QUART] for slab in (low, high) for i in range(3)], axis=1
        )
        value = base[half * HALF + start : half * HALF + start + QUART] + over_height(matmul(window, weights[...]))
        preact[cells] = value
        active = (value * jax.nn.sigmoid(value)).astype(bf16)
        hidden[cells] = active
        projected = matmul(active, proj[...])

        @pl.when(core == side)
        def _():
            keep[...] = projected

        @pl.when(core != side)
        def _():
            send[...] = projected.astype(bf16)


def prepare_kernel(
    below, centre, above, preact_a, preact_b, hidden_a, hidden_b, slope, hidden_t, features_t
):
    for q in range(4):
        cells = slice(q * QUART, (q + 1) * QUART)
        local = slice(q % 2 * QUART, (q % 2 + 1) * QUART)
        preact, hidden = ((preact_a, hidden_a), (preact_b, hidden_b))[q // 2]
        slope[cells] = silu_slope(preact[local])
        hidden_t[:, cells] = hidden[local].astype(f32).T.astype(bf16)
        for t, slab in enumerate((below, centre, above)):
            value = slab[cells].astype(f32)
            for j, moved in enumerate((from_below(value), value, from_above(value))):
                block = (t * 3 + j) * C
                features_t[block : block + C, cells] = moved.T.astype(bf16)


def output_kernel(half, row_ref, chip_sum, recv, bias, cot_mine, cot_pair, own, head):
    summed = chip_sum[...] + recv[...].astype(f32) + bias[...]
    head[...] = (summed * jax.nn.sigmoid(summed)).astype(bf16)
    cot = jnp.where(row_ref[0] == half, cot_mine[...], cot_pair[...])
    own[...] = (cot.astype(f32) * silu_slope(summed)).astype(bf16)


def gradient_kernel(
    core_ref, keep_ref, own_a, own_b, other_a, other_b, slope, proj, features_t, hidden_t,
    grads_out, d_pre_out, grads, d_pre, window, d_out, sems,
):
    d_pre[0:COL] = jnp.zeros((COL, F), bf16)
    d_pre[COL + ROWS : 2 * COL + ROWS] = jnp.zeros((COL, F), bf16)
    for q in range(4):
        start = q * QUART
        own, other = ((own_a, other_a), (own_b, other_b))[q // 2]
        rows = jnp.where(core_ref[0] == q % 2, own[...], other[...])
        d_out[start : start + QUART] = rows
        d_hidden = matmul_rt(rows, proj[...])
        d_pre[COL + start : COL + start + QUART] = (d_hidden * slope[start : start + QUART]).astype(bf16)
    copies = [pltpu.make_async_copy(d_pre, d_pre_out, sems.at[4])]
    copies[0].start()
    for i in range(3):
        window[:, i * F : (i + 1) * F] = d_pre[(2 - i) * COL : (2 - i) * COL + ROWS]
    grads[TAPS:] = matmul(hidden_t[...], d_out[...]).astype(bf16)
    spans = [(TAPS, F)] + [(t * 9 * C, 9 * C) for t in range(3)]

    def send_span(k):
        first, count = spans[k]
        copy = pltpu.make_async_copy(
            grads.at[first : first + count], grads_out.at[first : first + count], sems.at[k]
        )
        copy.start()
        copies.append(copy)

    send_span(0)
    off_centre = keep_ref[0]
    for t in range(3):
        block = matmul(features_t[t * 3 * C : (t + 1) * 3 * C], window[...])
        for i in range(3):
            for j in range(3):
                tap = (t * 9 + i * 3 + j) * C
                piece = block[j * C : (j + 1) * C, i * F : (i + 1) * F]
                if (t, i, j) != (1, 1, 1):
                    piece = piece * off_centre
                grads[tap : tap + C] = piece.astype(bf16)
        send_span(t + 1)
    for copy in copies:
        copy.wait()


def feature_kernel(d_pre, weights, low, mid, high):
    for q in range(4):
        start = q * QUART
        window = jnp.concatenate(
            [d_pre[start + (2 - i) * COL : start + (2 - i) * COL + QUART] for i in range(3)], axis=1
        )
        parts = matmul_rt(window, weights[...])
        total = parts[:, 3 * C : 6 * C] + from_above(parts[:, : 3 * C]) + from_below(parts[:, 6 * C :])
        cells = slice(start, start + QUART)
        low[cells] = total[:, :C].astype(bf16)
        mid[cells] = total[:, C : 2 * C]
        high[cells] = total[:, 2 * C :].astype(bf16)


def sum_of(parts):
    acc = parts[0].astype(f32)
    for k in range(1, parts.shape[0]):
        acc = acc + parts[k].astype(f32)
    return acc.astype(bf16)


def sum_kernel(parts, copies, total, sems):
    total[...] = sum_of(parts)
    peers = copies.shape[0]
    moves = [pltpu.make_async_copy(total, copies.at[k], sems.at[k]) for k in range(peers)]
    for move in moves:
        move.start()
    for move in moves:
        move.wait()


def widen_kernel(total, taps_out, proj_out, wide, sems):
    moves = []
    for k in range(4):
        first = k * TAPS // 4
        last = first + TAPS // 4
        wide[first:last] = total[first:last].astype(f32)
        moves.append(pltpu.make_async_copy(wide.at[first:last], taps_out.at[first:last], sems.at[k]))
        moves[-1].start()
    wide[TAPS:] = total[TAPS:].astype(f32)
    moves.append(pltpu.make_async_copy(wide.at[TAPS:], proj_out, sems.at[4]))
    moves[-1].start()
    for move in moves:
        move.wait()


def call(kernel, outs, specs, scratch, flops, *args, place=VMEM):
    return pl.pallas_call(
        kernel,
        out_shape=[jax.ShapeDtypeStruct(*o) for o in outs],
        in_specs=specs,
        out_specs=[place] * len(outs),
        scratch_shapes=scratch,
        compiler_params=pltpu.CompilerParams(vmem_limit_bytes=12 * 1024 * 1024),
        cost_estimate=pl.CostEstimate(flops=flops, bytes_accessed=8_000_000, transcendentals=0),
    )(*args)


def depth_pairs(mesh_gz, sign):
    strides = (0, 1, 2, 4)
    pairs = []
    for g in range(mesh_gz):
        for b in range(1, 4):
            target = g + sign * strides[b]
            if 0 <= target < mesh_gz:
                pairs.append((g * 4 + b, target * 4 + b))
    return pairs


def shards(slabs, features, tap_weights, branch_bias, proj_weights, out_bias, cotangent):
    branch = lax.axis_index(BR)
    core = lax.axis_index("c")
    row = lax.axis_index("yl")
    core_arg = core.astype(jnp.int32)[None]
    row_arg = row.astype(jnp.int32)[None]
    up = depth_pairs(slabs, 1)
    down = depth_pairs(slabs, -1)
    everywhere = GZ + BR
    proj = proj_weights[0]

    centre = lax.all_gather(features.reshape(QUART, C), BR, axis=0, tiled=True)
    tap = jnp.arange(27).reshape(3, 3, 3)
    off_centre = jnp.where(branch > 0, 1.0, 0.0).astype(f32)
    mask = jnp.where(tap == 13, 1.0, off_centre).astype(bf16)
    cot_mine = cotangent.reshape(QUART, F)
    centre, cot_mine = lax.optimization_barrier((centre, cot_mine))
    below = lax.ppermute(centre, everywhere, up)
    above = lax.ppermute(centre, everywhere, down)
    cot_pair = lax.ppermute(cot_mine, "yl", SWAP)
    masked = tap_weights[0] * mask[:, :, :, None, None]
    by_window = masked.transpose(0, 1, 3, 2, 4).reshape(3, 3 * C, 3 * F)
    weights_mid = by_window[1]
    weights_out = jnp.concatenate([by_window[0], by_window[2]], axis=0)
    weights_bwd = masked.transpose(2, 0, 3, 1, 4).reshape(9 * C, 3 * F)
    (base,) = call(
        centre_kernel,
        [((ROWS, F), f32)],
        [VMEM] * 3,
        [pltpu.VMEM((ROWS + 2 * COL, C), bf16)],
        2 * ROWS * 9 * C * F,
        centre, weights_mid, branch_bias,
    )
    below, above, cot_pair, base, weights_out, weights_bwd = lax.optimization_barrier(
        (below, above, cot_pair, base, weights_out, weights_bwd)
    )

    def forward_half(half):
        return call(
            functools.partial(forward_kernel, half),
            [((HALF, F), f32), ((HALF, F), bf16), ((QUART, F), f32), ((QUART, F), bf16)],
            [SMEM] + [VMEM] * 5,
            [pltpu.VMEM((HALF + 2 * COL, C), bf16)] * 2,
            ROWS * 18 * C * F,
            core_arg, below, above, weights_out, base, proj,
        )

    preact_a, hidden_a, keep_a, send_a = forward_half(0)
    chip_a = keep_a + lax.ppermute(send_a, "c", SWAP).astype(f32)
    preact_b, hidden_b, keep_b, send_b = forward_half(1)
    chip_send_a, send_b = lax.optimization_barrier((chip_a.astype(bf16), send_b))
    recv_a = lax.ppermute(chip_send_a, "yl", SWAP)
    chip_b = keep_b + lax.ppermute(send_b, "c", SWAP).astype(f32)
    chip_send_b, preact_b = lax.optimization_barrier((chip_b.astype(bf16), preact_b))
    recv_b = lax.ppermute(chip_send_b, "yl", SWAP)
    slope, hidden_t, features_t = call(
        prepare_kernel,
        [((ROWS, F), f32), ((F, ROWS), bf16), ((9 * C, ROWS), bf16)],
        [VMEM] * 7,
        [],
        2 * ROWS * 9 * C * F,
        below, centre, above, preact_a, preact_b, hidden_a, hidden_b,
    )
    recv_a, slope, hidden_t, features_t = lax.optimization_barrier((recv_a, slope, hidden_t, features_t))

    def output_half(half, chip_sum, recv):
        return call(
            functools.partial(output_kernel, half),
            [((QUART, F), bf16), ((QUART, F), bf16)],
            [SMEM] + [VMEM] * 5,
            [],
            1_000_000,
            row_arg, chip_sum, recv, out_bias[None], cot_mine, cot_pair,
        )

    own_a, head_a = output_half(0, chip_a, recv_a)
    own_a, recv_b = lax.optimization_barrier((own_a, recv_b))
    other_a = lax.ppermute(own_a, "c", SWAP)
    own_b, head_b = output_half(1, chip_b, recv_b)
    other_b = lax.ppermute(own_b, "c", SWAP)

    grads, d_pre = call(
        gradient_kernel,
        [((GRAD_ROWS, F), bf16), ((ROWS + 2 * COL, F), bf16)],
        [SMEM, SMEM] + [VMEM] * 8,
        [
            pltpu.VMEM((GRAD_ROWS, F), bf16),
            pltpu.VMEM((ROWS + 2 * COL, F), bf16),
            pltpu.VMEM((ROWS, 3 * F), bf16),
            pltpu.VMEM((ROWS, F), bf16),
            pltpu.SemaphoreType.DMA((5,)),
        ],
        2 * ROWS * 27 * C * F,
        core_arg, off_centre[None], own_a, own_b, other_a, other_b, slope, proj, features_t, hidden_t,
        place=HBM,
    )
    near = lax.axis_size("zl") * lax.axis_size("x") * lax.axis_size("yh")
    far = lax.axis_size("zh")
    share = GRAD_ROWS // near
    part = lax.all_to_all(grads.reshape(near, share, F), NEAR, 0, 0, tiled=True)
    low, mid, high = call(
        feature_kernel,
        [((ROWS, C), bf16), ((ROWS, C), f32), ((ROWS, C), bf16)],
        [VMEM] * 2,
        [],
        2 * ROWS * 27 * C * F,
        d_pre, weights_bwd,
    )

    def sum_for(peers, parts):
        return call(
            sum_kernel,
            [((peers, share, F), bf16)],
            [VMEM],
            [pltpu.VMEM((share, F), bf16), pltpu.SemaphoreType.DMA((peers,))],
            1_000_000,
            parts,
            place=HBM,
        )[0]

    part = sum_for(far, part)
    part, low, high = lax.optimization_barrier((part, low, high))
    part = lax.all_to_all(part, "zh", 0, 0, tiled=True)
    from_low = lax.ppermute(low, everywhere, down)
    from_high = lax.ppermute(high, everywhere, up)
    part = sum_for(near, part)
    part, mid, from_low, from_high = lax.optimization_barrier((part, mid, from_low, from_high))
    total = lax.all_to_all(part, NEAR, 0, 0, tiled=True).reshape(GRAD_ROWS, F)

    branch_grad = (mid + from_low.astype(f32) + from_high.astype(f32)).reshape(2, 2, QUART, C)
    sent = lax.dynamic_index_in_dim(branch_grad, 1 - core, 1, keepdims=False).astype(bf16)
    kept = lax.dynamic_index_in_dim(branch_grad, core, 1, keepdims=False)
    chip_grad = kept + lax.ppermute(sent, "c", SWAP).astype(f32)
    sent = lax.dynamic_index_in_dim(chip_grad, 1 - row, 0, keepdims=False).astype(bf16)
    kept = lax.dynamic_index_in_dim(chip_grad, row, 0, keepdims=False)
    feature_grad = (kept + lax.ppermute(sent, "yl", SWAP).astype(f32)).astype(bf16)
    head_out = jnp.where(row == 0, head_a, head_b)

    taps, proj_total = call(
        widen_kernel,
        [((TAPS, F), f32), ((F, F), f32)],
        [VMEM],
        [pltpu.VMEM((GRAD_ROWS, F), f32), pltpu.SemaphoreType.DMA((5,))],
        1_000_000,
        total,
        place=HBM,
    )
    return (
        head_out.reshape(cotangent.shape),
        feature_grad.reshape(features.shape),
        taps.reshape(1, 3, 3, 3, C, F),
        proj_total.reshape(1, F, F),
    )


def solution(mesh):
    slabs = mesh.shape["gz"]
    split = (4, 2, 4, 2) if slabs == 64 else (slabs, 1, 1, 1)
    fine = Mesh(mesh.devices.reshape(split + (2, 2)), GZ + BR)
    in_specs = (
        P(BR, GZ, None, None),
        P(BR, None, None, None, None, None),
        P(BR, None),
        P(BR, None, None),
        P(),
        P(BR, GZ, None, None),
    )
    out_specs = (
        P(BR, GZ, None, None),
        P(BR, GZ, None, None),
        P(BR, None, None, None, None, None),
        P(BR, None, None),
    )
    return jax.shard_map(
        functools.partial(shards, slabs), mesh=fine, in_specs=in_specs, out_specs=out_specs, check_vma=False
    )
```

```python
import functools
import math

import jax
import jax.numpy as jnp
from jax import lax
from jax.experimental import pallas as pl
from jax.experimental.pallas import tpu as pltpu
from jax.sharding import Mesh
from jax.sharding import PartitionSpec as P

C = 128
F = 256
COL = 64
ROWS = 2048
HALF = 1024
EARLY = 14 * COL
QUART = 512
TAPS = 27 * C
GRAD_ROWS = TAPS + F
bf16 = jnp.bfloat16
f32 = jnp.float32
GZ = ("zh", "zl", "x", "yh")
NEAR = ("zl", "x", "yh")
FAR = "zh"
BR = ("yl", "c")
SWAP = [(0, 1), (1, 0)]
VMEM = pl.BlockSpec(memory_space=pltpu.VMEM)
HBM = pl.BlockSpec(memory_space=pltpu.HBM)
SMEM = pl.BlockSpec(memory_space=pltpu.SMEM)


def silu_slope(values):
    logistic = jax.nn.sigmoid(values)
    return logistic * (1.0 + values * (1.0 - logistic))


def height_of(rows, lanes):
    return lax.broadcasted_iota(jnp.int32, (rows, lanes), 0) & 15


def from_below(values):
    rolled = pltpu.roll(values, 1, 0)
    return jnp.where(height_of(*values.shape) == 0, 0.0, rolled)


def from_above(values):
    rolled = pltpu.roll(values, values.shape[0] - 1, 0)
    return jnp.where(height_of(*values.shape) == 15, 0.0, rolled)


def matmul(lhs, rhs):
    return jnp.dot(lhs, rhs, preferred_element_type=f32)


def matmul_rt(lhs, rhs):
    return lax.dot_general(lhs, rhs, (((1,), (1,)), ((), ())), preferred_element_type=f32)


def pad_columns(padded, slab):
    padded[0:COL] = jnp.zeros((COL, C), bf16)
    padded[COL + ROWS : 2 * COL + ROWS] = jnp.zeros((COL, C), bf16)
    padded[COL : COL + ROWS] = slab[...]


def pad_half(padded, slab, half):
    if half == 0:
        padded[0:COL] = jnp.zeros((COL, C), bf16)
        padded[COL:] = slab[0 : HALF + COL]
    else:
        padded[0 : HALF + COL] = slab[HALF - COL :]
        padded[HALF + COL :] = jnp.zeros((COL, C), bf16)


def over_height(parts):
    return parts[:, F : 2 * F] + from_below(parts[:, :F]) + from_above(parts[:, 2 * F :])


def centre_kernel(centre, weights, bias, base, padded):
    pad_columns(padded, centre)
    for q in range(4):
        start = q * QUART
        window = jnp.concatenate([padded[start + i * COL : start + i * COL + QUART] for i in range(3)], axis=1)
        base[start : start + QUART] = bias[...] + over_height(matmul(window, weights[...]))


def forward_kernel(half, core_ref, below, above, weights, base, proj, preact, hidden, keep, send, low, high):
    pad_half(low, below, half)
    pad_half(high, above, half)
    core = core_ref[0]
    for side in range(2):
        start = side * QUART
        cells = slice(start, start + QUART)
        window = jnp.concatenate(
            [slab[start + i * COL : start + i * COL + QUART] for slab in (low, high) for i in range(3)], axis=1
        )
        value = base[half * HALF + start : half * HALF + start + QUART] + over_height(matmul(window, weights[...]))
        preact[cells] = value
        active = (value * jax.nn.sigmoid(value)).astype(bf16)
        hidden[cells] = active
        projected = matmul(active, proj[...])

        @pl.when(core == side)
        def _():
            keep[...] = projected

        @pl.when(core != side)
        def _():
            send[...] = projected.astype(bf16)


def prepare_kernel(
    below, centre, above, preact_a, preact_b, hidden_a, hidden_b, slope, hidden_t, features_t
):
    for q in range(4):
        cells = slice(q * QUART, (q + 1) * QUART)
        local = slice(q % 2 * QUART, (q % 2 + 1) * QUART)
        preact, hidden = ((preact_a, hidden_a), (preact_b, hidden_b))[q // 2]
        slope[cells] = silu_slope(preact[local])
        hidden_t[:, cells] = hidden[local].astype(f32).T.astype(bf16)
        for t, slab in enumerate((below, centre, above)):
            value = slab[cells].astype(f32)
            for j, moved in enumerate((from_below(value), value, from_above(value))):
                block = (t * 3 + j) * C
                features_t[block : block + C, cells] = moved.T.astype(bf16)


def output_kernel(half, row_ref, chip_sum, recv, bias, cot_mine, cot_pair, own, head):
    summed = chip_sum[...] + recv[...].astype(f32) + bias[...]
    head[...] = (summed * jax.nn.sigmoid(summed)).astype(bf16)
    cot = jnp.where(row_ref[0] == half, cot_mine[...], cot_pair[...])
    own[...] = (cot.astype(f32) * silu_slope(summed)).astype(bf16)


def height_sum(parts):
    return parts[:, 3 * C : 6 * C] + from_above(parts[:, : 3 * C]) + from_below(parts[:, 6 * C :])


def back_rows(core_ref, own, other, slope, proj, d_pre, at, d_out):
    for side in range(2):
        cells = slice(side * QUART, (side + 1) * QUART)
        rows = jnp.where(core_ref[0] == side, own[...], other[...])
        d_out[cells] = rows
        d_hidden = matmul_rt(rows, proj[...])
        d_pre[at + side * QUART : at + (side + 1) * QUART] = (d_hidden * slope[cells]).astype(bf16)


def back_features(d_pre, weights, start, count):
    window = jnp.concatenate(
        [d_pre[start + (2 - i) * COL : start + (2 - i) * COL + count] for i in range(3)], axis=1
    )
    return height_sum(matmul_rt(window, weights[...]))


def back_first_kernel(
    core_ref, own, other_0, other_1, slope, proj, weights, features_t, hidden_t,
    d_pre, low, mid, high, taps, projs, window, d_out, other,
):
    d_pre[0:COL] = jnp.zeros((COL, F), bf16)
    other[: QUART // 2] = other_0[...]
    other[QUART // 2 :] = other_1[...]
    back_rows(core_ref, own, other, slope, proj, d_pre, COL, d_out)
    for k in range(2):
        step = EARLY // 2
        total = back_features(d_pre, weights, k * step, step)
        cells = slice(k * step, (k + 1) * step)
        low[cells] = total[:, :C].astype(bf16)
        mid[cells] = total[:, C : 2 * C]
        high[cells] = total[:, 2 * C :].astype(bf16)
    for i in range(3):
        window[:, i * F : (i + 1) * F] = d_pre[(2 - i) * COL : (2 - i) * COL + EARLY]
    for t in range(3):
        rows = slice(t * 3 * C, (t + 1) * 3 * C)
        taps[rows] = matmul(features_t[rows, :EARLY], window[...])
    projs[...] = matmul(hidden_t[:, :HALF], d_out[...])


def back_second_kernel(
    core_ref, keep_ref, own, other, slope, proj, weights, features_t, hidden_t,
    d_pre_a, low_a, mid_a, high_a, taps, projs, low, mid, high, grads, d_pre, window, d_out,
):
    d_pre[0 : 3 * COL] = d_pre_a[HALF - 2 * COL :]
    d_pre[3 * COL + HALF :] = jnp.zeros((COL, F), bf16)
    back_rows(core_ref, own, other, slope.at[HALF:], proj, d_pre, 3 * COL, d_out)
    low[:EARLY] = low_a[...]
    mid[:EARLY] = mid_a[...]
    high[:EARLY] = high_a[...]
    late = ROWS - EARLY
    for k in range(3):
        step = late // 3
        total = back_features(d_pre, weights, k * step, step)
        cells = slice(EARLY + k * step, EARLY + (k + 1) * step)
        low[cells] = total[:, :C].astype(bf16)
        mid[cells] = total[:, C : 2 * C]
        high[cells] = total[:, 2 * C :].astype(bf16)
    for i in range(3):
        window[:, i * F : (i + 1) * F] = d_pre[(2 - i) * COL : (2 - i) * COL + late]
    off_centre = keep_ref[0]
    for t in range(3):
        rows = slice(t * 3 * C, (t + 1) * 3 * C)
        block = taps[rows] + matmul(features_t[rows, EARLY:], window[...])
        for i in range(3):
            for j in range(3):
                tap = (t * 9 + i * 3 + j) * C
                piece = block[j * C : (j + 1) * C, i * F : (i + 1) * F]
                if (t, i, j) != (1, 1, 1):
                    piece = piece * off_centre
                grads[tap : tap + C] = piece.astype(bf16)
    grads[TAPS:] = (projs[...] + matmul(hidden_t[:, HALF:], d_out[...])).astype(bf16)


def core_split_kernel(core_ref, low, mid, high, kept, sent):
    core = core_ref[0]
    for q in range(4):
        cells = slice(q * QUART, (q + 1) * QUART)
        total = mid[cells] + low[cells].astype(f32) + high[cells].astype(f32)

        @pl.when(core == q % 2)
        def _():
            kept[q // 2] = total

        @pl.when(core != q % 2)
        def _():
            sent[q // 2] = total.astype(bf16)


def chip_split_kernel(row_ref, kept, recv, mine, sent):
    row = row_ref[0]
    mine[...] = kept[row] + recv[row].astype(f32)
    sent[...] = (kept[1 - row] + recv[1 - row].astype(f32)).astype(bf16)


def sum_of(parts):
    acc = parts[0].astype(f32)
    for k in range(1, parts.shape[0]):
        acc = acc + parts[k].astype(f32)
    return acc.astype(bf16)


def sum_kernel(parts, copies, total, sems):
    total[...] = sum_of(parts)
    peers = copies.shape[0]
    moves = [pltpu.make_async_copy(total, copies.at[k], sems.at[k]) for k in range(peers)]
    for move in moves:
        move.start()
    for move in moves:
        move.wait()


def widen_kernel(total, taps_out, proj_out, wide, sems):
    moves = []
    for k in range(4):
        first = k * TAPS // 4
        last = first + TAPS // 4
        wide[first:last] = total[first:last].astype(f32)
        moves.append(pltpu.make_async_copy(wide.at[first:last], taps_out.at[first:last], sems.at[k]))
        moves[-1].start()
    wide[TAPS:] = total[TAPS:].astype(f32)
    moves.append(pltpu.make_async_copy(wide.at[TAPS:], proj_out, sems.at[4]))
    moves[-1].start()
    for move in moves:
        move.wait()


def call(kernel, outs, specs, scratch, flops, *args, place=VMEM):
    return pl.pallas_call(
        kernel,
        out_shape=[jax.ShapeDtypeStruct(*o) for o in outs],
        in_specs=specs,
        out_specs=[place] * len(outs),
        scratch_shapes=scratch,
        compiler_params=pltpu.CompilerParams(vmem_limit_bytes=12 * 1024 * 1024),
        cost_estimate=pl.CostEstimate(flops=flops, bytes_accessed=flops // 1000, transcendentals=0),
    )(*args)


def depth_pairs(mesh_gz, sign):
    strides = (0, 1, 2, 4)
    pairs = []
    for g in range(mesh_gz):
        for b in range(1, 4):
            target = g + sign * strides[b]
            if 0 <= target < mesh_gz:
                pairs.append((g * 4 + b, target * 4 + b))
    return pairs


def shards(slabs, features, tap_weights, branch_bias, proj_weights, out_bias, cotangent):
    branch = lax.axis_index(BR)
    core = lax.axis_index("c")
    row = lax.axis_index("yl")
    core_arg = core.astype(jnp.int32)[None]
    row_arg = row.astype(jnp.int32)[None]
    up = depth_pairs(slabs, 1)
    down = depth_pairs(slabs, -1)
    everywhere = GZ + BR
    proj = proj_weights[0]

    centre = lax.all_gather(features.reshape(QUART, C), BR, axis=0, tiled=True)
    tap = jnp.arange(27).reshape(3, 3, 3)
    off_centre = jnp.where(branch > 0, 1.0, 0.0).astype(f32)
    mask = jnp.where(tap == 13, 1.0, off_centre).astype(bf16)
    cot_mine = cotangent.reshape(QUART, F)
    centre, cot_mine = lax.optimization_barrier((centre, cot_mine))
    below = lax.ppermute(centre, everywhere, up)
    above = lax.ppermute(centre, everywhere, down)
    cot_pair = lax.ppermute(cot_mine, "yl", SWAP)
    masked = tap_weights[0] * mask[:, :, :, None, None]
    by_window = masked.transpose(0, 1, 3, 2, 4).reshape(3, 3 * C, 3 * F)
    weights_mid = by_window[1]
    weights_out = jnp.concatenate([by_window[0], by_window[2]], axis=0)
    weights_bwd = masked.transpose(2, 0, 3, 1, 4).reshape(9 * C, 3 * F)
    (base,) = call(
        centre_kernel,
        [((ROWS, F), f32)],
        [VMEM] * 3,
        [pltpu.VMEM((ROWS + 2 * COL, C), bf16)],
        2 * ROWS * 9 * C * F,
        centre, weights_mid, branch_bias,
    )
    below, above, cot_pair, base, weights_out, weights_bwd = lax.optimization_barrier(
        (below, above, cot_pair, base, weights_out, weights_bwd)
    )

    def forward_half(half):
        return call(
            functools.partial(forward_kernel, half),
            [((HALF, F), f32), ((HALF, F), bf16), ((QUART, F), f32), ((QUART, F), bf16)],
            [SMEM] + [VMEM] * 5,
            [pltpu.VMEM((HALF + 2 * COL, C), bf16)] * 2,
            ROWS * 18 * C * F,
            core_arg, below, above, weights_out, base, proj,
        )

    preact_a, hidden_a, keep_a, send_a = forward_half(0)
    chip_a = keep_a + lax.ppermute(send_a, "c", SWAP).astype(f32)
    preact_b, hidden_b, keep_b, send_b = forward_half(1)
    chip_send_a, send_b = lax.optimization_barrier((chip_a.astype(bf16), send_b))
    recv_a = lax.ppermute(chip_send_a, "yl", SWAP)
    chip_b = keep_b + lax.ppermute(send_b, "c", SWAP).astype(f32)
    chip_send_b, preact_b = lax.optimization_barrier((chip_b.astype(bf16), preact_b))
    recv_b = lax.ppermute(chip_send_b, "yl", SWAP)
    slope, hidden_t, features_t = call(
        prepare_kernel,
        [((ROWS, F), f32), ((F, ROWS), bf16), ((9 * C, ROWS), bf16)],
        [VMEM] * 7,
        [],
        1000,
        below, centre, above, preact_a, preact_b, hidden_a, hidden_b,
    )
    recv_a, slope, hidden_t, features_t = lax.optimization_barrier((recv_a, slope, hidden_t, features_t))

    def output_half(half, chip_sum, recv):
        return call(
            functools.partial(output_kernel, half),
            [((QUART, F), bf16), ((QUART, F), bf16)],
            [SMEM] + [VMEM] * 5,
            [],
            1000,
            row_arg, chip_sum, recv, out_bias[None], cot_mine, cot_pair,
        )

    own_a, head_a = output_half(0, chip_a, recv_a)
    other_a = [lax.ppermute(own_a[k : k + QUART // 2], "c", SWAP) for k in (0, QUART // 2)]
    d_pre_a, low_a, mid_a, high_a, taps_a, projs_a = call(
        back_first_kernel,
        [
            ((HALF + COL, F), bf16),
            ((EARLY, C), bf16),
            ((EARLY, C), f32),
            ((EARLY, C), bf16),
            ((9 * C, 3 * F), f32),
            ((F, F), f32),
        ],
        [SMEM] + [VMEM] * 8,
        [pltpu.VMEM((EARLY, 3 * F), bf16), pltpu.VMEM((HALF, F), bf16), pltpu.VMEM((QUART, F), bf16)],
        1000,
        core_arg, own_a, *other_a, slope, proj, weights_bwd, features_t, hidden_t,
    )
    recv_b, taps_a, d_pre_a = lax.optimization_barrier((recv_b, taps_a, d_pre_a))
    own_b, head_b = output_half(1, chip_b, recv_b)
    other_b = lax.ppermute(own_b, "c", SWAP)
    low, mid, high, grads = call(
        back_second_kernel,
        [((ROWS, C), bf16), ((ROWS, C), f32), ((ROWS, C), bf16), ((GRAD_ROWS, F), bf16)],
        [SMEM, SMEM] + [VMEM] * 13,
        [
            pltpu.VMEM((HALF + 4 * COL, F), bf16),
            pltpu.VMEM((ROWS - EARLY, 3 * F), bf16),
            pltpu.VMEM((HALF, F), bf16),
        ],
        2 * ROWS * 27 * C * F,
        core_arg, off_centre[None], own_b, other_b, slope, proj, weights_bwd, features_t, hidden_t,
        d_pre_a, low_a, mid_a, high_a, taps_a, projs_a,
    )
    head_out = jnp.where(row == 0, head_a, head_b)
    near = math.prod(lax.axis_size(a) for a in NEAR)
    far = lax.axis_size(FAR)
    share = GRAD_ROWS // near
    grads, low, mid, high = lax.optimization_barrier((grads, low, mid, high))
    part = lax.all_to_all(grads.reshape(near, share, F), NEAR, 0, 0, tiled=True)
    part, low, mid, high = lax.optimization_barrier((part, low, mid, high))

    def sum_for(peers, parts):
        return call(
            sum_kernel,
            [((peers, share, F), bf16)],
            [VMEM],
            [pltpu.VMEM((share, F), bf16), pltpu.SemaphoreType.DMA((peers,))],
            1_000_000,
            parts,
            place=HBM,
        )[0]

    part = sum_for(far, part)
    part, low, high = lax.optimization_barrier((part, low, high))
    from_low = lax.ppermute(low, everywhere, down)
    from_high = lax.ppermute(high, everywhere, up)
    part = lax.all_to_all(part, FAR, 0, 0, tiled=True)
    part = sum_for(near, part)

    kept, sent = call(
        core_split_kernel,
        [((2, QUART, C), f32), ((2, QUART, C), bf16)],
        [SMEM] + [VMEM] * 3,
        [],
        1_000_000,
        core_arg, from_low, mid, from_high,
    )
    mine, sent = call(
        chip_split_kernel,
        [((QUART, C), f32), ((QUART, C), bf16)],
        [SMEM] + [VMEM] * 2,
        [],
        1_000_000,
        row_arg, kept, lax.ppermute(sent, "c", SWAP),
    )
    feature_grad = (mine + lax.ppermute(sent, "yl", SWAP).astype(f32)).astype(bf16)
    part, feature_grad, head_out = lax.optimization_barrier((part, feature_grad, head_out))
    total = lax.all_to_all(part, NEAR, 0, 0, tiled=True).reshape(GRAD_ROWS, F)

    taps, proj_total = call(
        widen_kernel,
        [((TAPS, F), f32), ((F, F), f32)],
        [VMEM],
        [pltpu.VMEM((GRAD_ROWS, F), f32), pltpu.SemaphoreType.DMA((5,))],
        1_000_000,
        total,
        place=HBM,
    )
    return (
        head_out.reshape(cotangent.shape),
        feature_grad.reshape(features.shape),
        taps.reshape(1, 3, 3, 3, C, F),
        proj_total.reshape(1, F, F),
    )


def solution(mesh):
    slabs = mesh.shape["gz"]
    split = (4, 2, 4, 2) if slabs == 64 else (slabs, 1, 1, 1)
    fine = Mesh(mesh.devices.reshape(split + (2, 2)), GZ + BR)
    in_specs = (
        P(BR, GZ, None, None),
        P(BR, None, None, None, None, None),
        P(BR, None),
        P(BR, None, None),
        P(),
        P(BR, GZ, None, None),
    )
    out_specs = (
        P(BR, GZ, None, None),
        P(BR, GZ, None, None),
        P(BR, None, None, None, None, None),
        P(BR, None, None),
    )
    return jax.shard_map(
        functools.partial(shards, slabs), mesh=fine, in_specs=in_specs, out_specs=out_specs, check_vma=False
    )
```

```python
import functools
import math

import jax
import jax.numpy as jnp
from jax import lax
from jax.experimental import pallas as pl
from jax.experimental.pallas import tpu as pltpu
from jax.sharding import Mesh
from jax.sharding import PartitionSpec as P

C = 128
F = 256
COL = 64
ROWS = 2048
HALF = 1024
EARLY = 12 * COL
QUART = 512
TAPS = 27 * C
GRAD_ROWS = TAPS + F
bf16 = jnp.bfloat16
f32 = jnp.float32
GZ = ("zh", "zl", "x", "yh")
NEAR = ("zl", "x", "yh")
FAR = "zh"
BR = ("yl", "c")
SWAP = [(0, 1), (1, 0)]
VMEM = pl.BlockSpec(memory_space=pltpu.VMEM)
HBM = pl.BlockSpec(memory_space=pltpu.HBM)
SMEM = pl.BlockSpec(memory_space=pltpu.SMEM)


def silu_slope(values):
    logistic = jax.nn.sigmoid(values)
    return logistic * (1.0 + values * (1.0 - logistic))


def height_of(rows, lanes):
    return lax.broadcasted_iota(jnp.int32, (rows, lanes), 0) & 15


def from_below(values):
    rolled = pltpu.roll(values, 1, 0)
    return jnp.where(height_of(*values.shape) == 0, 0.0, rolled)


def from_above(values):
    rolled = pltpu.roll(values, values.shape[0] - 1, 0)
    return jnp.where(height_of(*values.shape) == 15, 0.0, rolled)


def matmul(lhs, rhs):
    return jnp.dot(lhs, rhs, preferred_element_type=f32)


def matmul_rt(lhs, rhs):
    return lax.dot_general(lhs, rhs, (((1,), (1,)), ((), ())), preferred_element_type=f32)


def pad_columns(padded, slab):
    padded[0:COL] = jnp.zeros((COL, C), bf16)
    padded[COL + ROWS : 2 * COL + ROWS] = jnp.zeros((COL, C), bf16)
    padded[COL : COL + ROWS] = slab[...]


def pad_half(padded, slab, half):
    if half == 0:
        padded[0:COL] = jnp.zeros((COL, C), bf16)
        padded[COL:] = slab[0 : HALF + COL]
    else:
        padded[0 : HALF + COL] = slab[HALF - COL :]
        padded[HALF + COL :] = jnp.zeros((COL, C), bf16)


def over_height(parts):
    return parts[:, F : 2 * F] + from_below(parts[:, :F]) + from_above(parts[:, 2 * F :])


def centre_kernel(centre, weights, bias, base, padded):
    pad_columns(padded, centre)
    for q in range(4):
        start = q * QUART
        window = jnp.concatenate([padded[start + i * COL : start + i * COL + QUART] for i in range(3)], axis=1)
        base[start : start + QUART] = bias[...] + over_height(matmul(window, weights[...]))


def forward_kernel(
    half, core_ref, below, above, weights, base, proj, preact, hidden, keep, send_0, send_1, low, high, sides
):
    pad_half(low, below, half)
    pad_half(high, above, half)
    for side in range(2):
        start = side * QUART
        cells = slice(start, start + QUART)
        window = jnp.concatenate(
            [slab[start + i * COL : start + i * COL + QUART] for slab in (low, high) for i in range(3)], axis=1
        )
        value = base[half * HALF + start : half * HALF + start + QUART] + over_height(matmul(window, weights[...]))
        preact[cells] = value
        active = (value * jax.nn.sigmoid(value)).astype(bf16)
        hidden[cells] = active
        sides[side] = matmul(active, proj[...])
    core = core_ref[0]
    keep[...] = sides[core]
    send_0[...] = sides[1 - core, : QUART // 2].astype(bf16)
    send_1[...] = sides[1 - core, QUART // 2 :].astype(bf16)


def prepare_kernel(
    below, centre, above, preact_a, preact_b, hidden_a, hidden_b, slope, hidden_t, features_t
):
    for q in range(4):
        cells = slice(q * QUART, (q + 1) * QUART)
        local = slice(q % 2 * QUART, (q % 2 + 1) * QUART)
        preact, hidden = ((preact_a, hidden_a), (preact_b, hidden_b))[q // 2]
        slope[cells] = silu_slope(preact[local])
        hidden_t[:, cells] = hidden[local].astype(f32).T.astype(bf16)
        for t, slab in enumerate((below, centre, above)):
            value = slab[cells].astype(f32)
            for j, moved in enumerate((from_below(value), value, from_above(value))):
                block = (t * 3 + j) * C
                features_t[block : block + C, cells] = moved.T.astype(bf16)


def d_out_of(summed, cot):
    return (cot.astype(f32) * silu_slope(summed)).astype(bf16)


def head_of(summed):
    return (summed * jax.nn.sigmoid(summed)).astype(bf16)


def first_output_kernel(row_ref, chip_sum, recv, bias, cot_mine, cot_pair, own_0, own_1):
    for k, own in enumerate((own_0, own_1)):
        cells = slice(k * (QUART // 2), (k + 1) * (QUART // 2))
        summed = chip_sum[cells] + recv[cells].astype(f32) + bias[...]
        own[...] = d_out_of(summed, jnp.where(row_ref[0] == 0, cot_mine[cells], cot_pair[cells]))


def second_output_kernel(row_ref, chip_sum, recv, bias, cot_mine, cot_pair, own):
    summed = chip_sum[...] + recv[...].astype(f32) + bias[...]
    own[...] = d_out_of(summed, jnp.where(row_ref[0] == 1, cot_mine[...], cot_pair[...]))


def head_kernel(row_ref, chip_a, recv_a, chip_b, recv_b, bias, head):
    first = row_ref[0] == 0
    partial = jnp.where(first, chip_a[...], chip_b[...])
    head[...] = head_of(partial + jnp.where(first, recv_a[...], recv_b[...]).astype(f32) + bias[...])


def height_sum(parts):
    return parts[:, 3 * C : 6 * C] + from_above(parts[:, : 3 * C]) + from_below(parts[:, 6 * C :])


def back_rows(core_ref, own, other, slope, proj, d_pre, at, d_out):
    for side in range(2):
        start = side * QUART
        for mine, theirs in zip(own, other):
            count = mine.shape[0]
            rows = jnp.where(core_ref[0] == side, mine[...], theirs[...])
            d_out[start : start + count] = rows
            d_hidden = matmul_rt(rows, proj[...])
            d_pre[at + start : at + start + count] = (d_hidden * slope[start : start + count]).astype(bf16)
            start += count


def back_features(d_pre, weights, start, count):
    window = jnp.concatenate(
        [d_pre[start + (2 - i) * COL : start + (2 - i) * COL + count] for i in range(3)], axis=1
    )
    return height_sum(matmul_rt(window, weights[...]))


def back_first_kernel(
    core_ref, own_0, own_1, other_0, other_1, slope, proj, weights, features_t, hidden_t,
    d_pre, low, mid, high, taps, projs, window, d_out,
):
    d_pre[0:COL] = jnp.zeros((COL, F), bf16)
    back_rows(core_ref, (own_0, own_1), (other_0, other_1), slope, proj, d_pre, COL, d_out)
    for k in range(2):
        step = EARLY // 2
        total = back_features(d_pre, weights, k * step, step)
        cells = slice(k * step, (k + 1) * step)
        low[cells] = total[:, :C].astype(bf16)
        mid[cells] = total[:, C : 2 * C]
        high[cells] = total[:, 2 * C :].astype(bf16)
    for i in range(3):
        window[:, i * F : (i + 1) * F] = d_pre[(2 - i) * COL : (2 - i) * COL + EARLY]
    for t in range(3):
        rows = slice(t * 3 * C, (t + 1) * 3 * C)
        taps[rows] = matmul(features_t[rows, :EARLY], window[...])
    projs[...] = matmul(hidden_t[:, :HALF], d_out[...])


def back_second_kernel(
    core_ref, keep_ref, own, other, slope, proj, weights, features_t, hidden_t,
    d_pre_a, low_a, mid_a, high_a, taps, projs, low, mid, high, grads, d_pre, window, d_out,
):
    d_pre[0 : 5 * COL] = d_pre_a[HALF - 4 * COL :]
    d_pre[5 * COL + HALF :] = jnp.zeros((COL, F), bf16)
    back_rows(core_ref, (own,), (other,), slope.at[HALF:], proj, d_pre, 5 * COL, d_out)
    low[:EARLY] = low_a[...]
    mid[:EARLY] = mid_a[...]
    high[:EARLY] = high_a[...]
    late = ROWS - EARLY
    for k in range(2):
        step = late // 2
        total = back_features(d_pre, weights, k * step, step)
        cells = slice(EARLY + k * step, EARLY + (k + 1) * step)
        low[cells] = total[:, :C].astype(bf16)
        mid[cells] = total[:, C : 2 * C]
        high[cells] = total[:, 2 * C :].astype(bf16)
    for i in range(3):
        window[:, i * F : (i + 1) * F] = d_pre[(2 - i) * COL : (2 - i) * COL + late]
    off_centre = keep_ref[0]
    for t in range(3):
        rows = slice(t * 3 * C, (t + 1) * 3 * C)
        block = taps[rows] + matmul(features_t[rows, EARLY:], window[...])
        for i in range(3):
            for j in range(3):
                tap = (t * 9 + i * 3 + j) * C
                piece = block[j * C : (j + 1) * C, i * F : (i + 1) * F]
                if (t, i, j) != (1, 1, 1):
                    piece = piece * off_centre
                grads[tap : tap + C] = piece.astype(bf16)
    grads[TAPS:] = (projs[...] + matmul(hidden_t[:, HALF:], d_out[...])).astype(bf16)


def core_split_kernel(core_ref, low, mid, high, kept, sent, total):
    for q in range(4):
        cells = slice(q * QUART, (q + 1) * QUART)
        total[q] = mid[cells] + low[cells].astype(f32) + high[cells].astype(f32)
    core = core_ref[0]
    for row in range(2):
        kept[row] = total[2 * row + core]
        sent[row] = total[2 * row + 1 - core].astype(bf16)


def chip_split_kernel(row_ref, kept, recv, mine, sent):
    row = row_ref[0]
    mine[...] = kept[row] + recv[row].astype(f32)
    sent[...] = (kept[1 - row] + recv[1 - row].astype(f32)).astype(bf16)


def sum_of(parts):
    acc = parts[0].astype(f32)
    for k in range(1, parts.shape[0]):
        acc = acc + parts[k].astype(f32)
    return acc.astype(bf16)


def sum_kernel(parts, copies):
    total = sum_of(parts)
    for k in range(copies.shape[0]):
        copies[k] = total


def widen_kernel(total, taps_out, proj_out, wide, sems):
    moves = []
    for k in range(4):
        first = k * TAPS // 4
        last = first + TAPS // 4
        wide[first:last] = total[first:last].astype(f32)
        moves.append(pltpu.make_async_copy(wide.at[first:last], taps_out.at[first:last], sems.at[k]))
        moves[-1].start()
    wide[TAPS:] = total[TAPS:].astype(f32)
    moves.append(pltpu.make_async_copy(wide.at[TAPS:], proj_out, sems.at[4]))
    moves[-1].start()
    for move in moves:
        move.wait()


def call(kernel, outs, specs, scratch, flops, *args, place=VMEM):
    return pl.pallas_call(
        kernel,
        out_shape=[jax.ShapeDtypeStruct(*o) for o in outs],
        in_specs=specs,
        out_specs=[place] * len(outs),
        scratch_shapes=scratch,
        compiler_params=pltpu.CompilerParams(vmem_limit_bytes=12 * 1024 * 1024),
        cost_estimate=pl.CostEstimate(flops=flops, bytes_accessed=flops // 1000, transcendentals=0),
    )(*args)


def depth_pairs(mesh_gz, sign):
    strides = (0, 1, 2, 4)
    pairs = []
    for g in range(mesh_gz):
        for b in range(1, 4):
            target = g + sign * strides[b]
            if 0 <= target < mesh_gz:
                pairs.append((g * 4 + b, target * 4 + b))
    return pairs


def exchanged(parts, axis):
    return jnp.concatenate([lax.ppermute(part, axis, SWAP) for part in parts], axis=0).astype(f32)


def shards(slabs, features, tap_weights, branch_bias, proj_weights, out_bias, cotangent):
    branch = lax.axis_index(BR)
    core = lax.axis_index("c")
    row = lax.axis_index("yl")
    core_arg = core.astype(jnp.int32)[None]
    row_arg = row.astype(jnp.int32)[None]
    up = depth_pairs(slabs, 1)
    down = depth_pairs(slabs, -1)
    everywhere = GZ + BR
    proj = proj_weights[0]

    centre = lax.all_gather(features.reshape(QUART, C), BR, axis=0, tiled=True)
    tap = jnp.arange(27).reshape(3, 3, 3)
    off_centre = jnp.where(branch > 0, 1.0, 0.0).astype(f32)
    mask = jnp.where(tap == 13, 1.0, off_centre).astype(bf16)
    cot_mine = cotangent.reshape(QUART, F)
    centre, cot_mine = lax.optimization_barrier((centre, cot_mine))
    below = lax.ppermute(centre, everywhere, up)
    above = lax.ppermute(centre, everywhere, down)
    cot_pair = lax.ppermute(cot_mine, "yl", SWAP)
    masked = tap_weights[0] * mask[:, :, :, None, None]
    by_window = masked.transpose(0, 1, 3, 2, 4).reshape(3, 3 * C, 3 * F)
    weights_mid = by_window[1]
    weights_out = jnp.concatenate([by_window[0], by_window[2]], axis=0)
    weights_bwd = masked.transpose(2, 0, 3, 1, 4).reshape(9 * C, 3 * F)
    (base,) = call(
        centre_kernel,
        [((ROWS, F), f32)],
        [VMEM] * 3,
        [pltpu.VMEM((ROWS + 2 * COL, C), bf16)],
        2 * ROWS * 9 * C * F,
        centre, weights_mid, branch_bias,
    )
    below, above, cot_pair, base, weights_out, weights_bwd = lax.optimization_barrier(
        (below, above, cot_pair, base, weights_out, weights_bwd)
    )

    def forward_half(half, base):
        return call(
            functools.partial(forward_kernel, half),
            [((HALF, F), f32), ((HALF, F), bf16), ((QUART, F), f32)] + [((QUART // 2, F), bf16)] * 2,
            [SMEM] + [VMEM] * 5,
            [pltpu.VMEM((HALF + 2 * COL, C), bf16)] * 2 + [pltpu.VMEM((2, QUART, F), f32)],
            1000,
            core_arg, below, above, weights_out, base, proj,
        )

    preact_a, hidden_a, keep_a, *send_a = forward_half(0, base)
    chip_a = keep_a + exchanged(send_a, "c")
    preact_b, hidden_b, keep_b, *send_b = forward_half(1, base)
    chip_send_a, *send_b = lax.optimization_barrier((chip_a.astype(bf16), *send_b))
    recv_a = lax.ppermute(chip_send_a, "yl", SWAP)
    chip_b = keep_b + exchanged(send_b, "c")
    chip_send_b, preact_b = lax.optimization_barrier((chip_b.astype(bf16), preact_b))
    recv_b = lax.ppermute(chip_send_b, "yl", SWAP)
    slope, hidden_t, features_t = call(
        prepare_kernel,
        [((ROWS, F), f32), ((F, ROWS), bf16), ((9 * C, ROWS), bf16)],
        [VMEM] * 7,
        [],
        1000,
        below, centre, above, preact_a, preact_b, hidden_a, hidden_b,
    )
    recv_a, slope, hidden_t, features_t = lax.optimization_barrier((recv_a, slope, hidden_t, features_t))

    own_a = call(
        first_output_kernel,
        [((QUART // 2, F), bf16), ((QUART // 2, F), bf16)],
        [SMEM] + [VMEM] * 5,
        [],
        1000,
        row_arg, chip_a, recv_a, out_bias[None], cot_mine, cot_pair,
    )
    other_a = [lax.ppermute(part, "c", SWAP) for part in own_a]
    d_pre_a, low_a, mid_a, high_a, taps_a, projs_a = call(
        back_first_kernel,
        [
            ((HALF + COL, F), bf16),
            ((EARLY, C), bf16),
            ((EARLY, C), f32),
            ((EARLY, C), bf16),
            ((9 * C, 3 * F), f32),
            ((F, F), f32),
        ],
        [SMEM] + [VMEM] * 9,
        [pltpu.VMEM((EARLY, 3 * F), bf16), pltpu.VMEM((HALF, F), bf16)],
        1000,
        core_arg, *own_a, *other_a, slope, proj, weights_bwd, features_t, hidden_t,
    )
    recv_b, taps_a, d_pre_a = lax.optimization_barrier((recv_b, taps_a, d_pre_a))
    (own_b,) = call(
        second_output_kernel,
        [((QUART, F), bf16)],
        [SMEM] + [VMEM] * 5,
        [],
        1000,
        row_arg, chip_b, recv_b, out_bias[None], cot_mine, cot_pair,
    )
    other_b = lax.ppermute(own_b, "c", SWAP)
    low, mid, high, grads = call(
        back_second_kernel,
        [((ROWS, C), bf16), ((ROWS, C), f32), ((ROWS, C), bf16), ((GRAD_ROWS, F), bf16)],
        [SMEM, SMEM] + [VMEM] * 13,
        [
            pltpu.VMEM((HALF + 6 * COL, F), bf16),
            pltpu.VMEM((ROWS - EARLY, 3 * F), bf16),
            pltpu.VMEM((HALF, F), bf16),
        ],
        2 * ROWS * 27 * C * F,
        core_arg, off_centre[None], own_b, other_b, slope, proj, weights_bwd, features_t, hidden_t,
        d_pre_a, low_a, mid_a, high_a, taps_a, projs_a,
    )
    near = math.prod(lax.axis_size(a) for a in NEAR)
    far = lax.axis_size(FAR)
    share = GRAD_ROWS // near
    grads, low, mid, high = lax.optimization_barrier((grads, low, mid, high))
    part = lax.all_to_all(grads.reshape(near, share, F), NEAR, 0, 0, tiled=True)
    part, low, mid, high = lax.optimization_barrier((part, low, mid, high))

    def sum_for(peers, parts):
        return call(
            sum_kernel,
            [((peers, share, F), bf16)],
            [VMEM],
            [],
            1_000_000,
            parts,
        )[0]

    part = sum_for(far, part)
    part, low, high, chip_a = lax.optimization_barrier((part, low, high, chip_a))
    (head_out,) = call(
        head_kernel,
        [((QUART, F), bf16)],
        [SMEM] + [VMEM] * 5,
        [],
        1000,
        row_arg, chip_a, recv_a, chip_b, recv_b, out_bias[None],
    )
    from_low = lax.ppermute(low, everywhere, down)
    from_high = lax.ppermute(high, everywhere, up)
    part = lax.all_to_all(part, FAR, 0, 0, tiled=True)
    part = sum_for(near, part)

    kept, sent = call(
        core_split_kernel,
        [((2, QUART, C), f32), ((2, QUART, C), bf16)],
        [SMEM] + [VMEM] * 3,
        [pltpu.VMEM((4, QUART, C), f32)],
        1_000_000,
        core_arg, from_low, mid, from_high,
    )
    mine, sent = call(
        chip_split_kernel,
        [((QUART, C), f32), ((QUART, C), bf16)],
        [SMEM] + [VMEM] * 2,
        [],
        1_000_000,
        row_arg, kept, lax.ppermute(sent, "c", SWAP),
    )
    recv = lax.ppermute(sent, "yl", SWAP)
    feature_grad = (mine + recv.astype(f32)).astype(bf16)
    part, feature_grad, head_out = lax.optimization_barrier((part, feature_grad, head_out))
    total = lax.all_to_all(part, NEAR, 0, 0, tiled=True).reshape(GRAD_ROWS, F)
    taps, proj_total = call(
        widen_kernel,
        [((TAPS, F), f32), ((F, F), f32)],
        [VMEM],
        [pltpu.VMEM((GRAD_ROWS, F), f32), pltpu.SemaphoreType.DMA((5,))],
        1_000_000,
        total,
        place=HBM,
    )
    return (
        head_out.reshape(cotangent.shape),
        feature_grad.reshape(features.shape),
        taps.reshape(1, 3, 3, 3, C, F),
        proj_total.reshape(1, F, F),
    )


def solution(mesh):
    slabs = mesh.shape["gz"]
    split = (4, 2, 4, 2) if slabs == 64 else (slabs, 1, 1, 1)
    fine = Mesh(mesh.devices.reshape(split + (2, 2)), GZ + BR)
    in_specs = (
        P(BR, GZ, None, None),
        P(BR, None, None, None, None, None),
        P(BR, None),
        P(BR, None, None),
        P(),
        P(BR, GZ, None, None),
    )
    out_specs = (
        P(BR, GZ, None, None),
        P(BR, GZ, None, None),
        P(BR, None, None, None, None, None),
        P(BR, None, None),
    )
    return jax.shard_map(
        functools.partial(shards, slabs), mesh=fine, in_specs=in_specs, out_specs=out_specs, check_vma=False
    )
```

```python
import functools
import math

import jax
import jax.numpy as jnp
from jax import lax
from jax.experimental import pallas as pl
from jax.experimental.pallas import tpu as pltpu
from jax.sharding import Mesh
from jax.sharding import PartitionSpec as P

C = 128
F = 256
COL = 64
ROWS = 2048
HALF = 1024
EARLY = 12 * COL
QUART = 512
TAPS = 27 * C
GRAD_ROWS = TAPS + F
bf16 = jnp.bfloat16
f32 = jnp.float32
GZ = ("zh", "zl", "x", "yh")
NEAR = ("zl", "x", "yh")
FAR = "zh"
BR = ("yl", "c")
SWAP = [(0, 1), (1, 0)]
VMEM = pl.BlockSpec(memory_space=pltpu.VMEM)
HBM = pl.BlockSpec(memory_space=pltpu.HBM)
SMEM = pl.BlockSpec(memory_space=pltpu.SMEM)


def silu_slope(values):
    logistic = jax.nn.sigmoid(values)
    return logistic * (1.0 + values * (1.0 - logistic))


def height_of(rows, lanes):
    return lax.broadcasted_iota(jnp.int32, (rows, lanes), 0) & 15


def from_below(values):
    rolled = pltpu.roll(values, 1, 0)
    return jnp.where(height_of(*values.shape) == 0, 0.0, rolled)


def from_above(values):
    rolled = pltpu.roll(values, values.shape[0] - 1, 0)
    return jnp.where(height_of(*values.shape) == 15, 0.0, rolled)


def matmul(lhs, rhs):
    return jnp.dot(lhs, rhs, preferred_element_type=f32)


def matmul_rt(lhs, rhs):
    return lax.dot_general(lhs, rhs, (((1,), (1,)), ((), ())), preferred_element_type=f32)


def pad_columns(padded, slab):
    padded[0:COL] = jnp.zeros((COL, C), bf16)
    padded[COL + ROWS : 2 * COL + ROWS] = jnp.zeros((COL, C), bf16)
    padded[COL : COL + ROWS] = slab[...]


def pad_half(padded, slab, half):
    if half == 0:
        padded[0:COL] = jnp.zeros((COL, C), bf16)
        padded[COL:] = slab[0 : HALF + COL]
    else:
        padded[0 : HALF + COL] = slab[HALF - COL :]
        padded[HALF + COL :] = jnp.zeros((COL, C), bf16)


def over_height(parts):
    return parts[:, F : 2 * F] + from_below(parts[:, :F]) + from_above(parts[:, 2 * F :])


def centre_kernel(centre, weights, bias, base, padded):
    pad_columns(padded, centre)
    for q in range(4):
        start = q * QUART
        window = jnp.concatenate([padded[start + i * COL : start + i * COL + QUART] for i in range(3)], axis=1)
        base[start : start + QUART] = bias[...] + over_height(matmul(window, weights[...]))


def forward_kernel(
    half, core_ref, below, above, weights, base, proj, preact, hidden, keep, send_0, send_1, low, high, sides
):
    pad_half(low, below, half)
    pad_half(high, above, half)
    for side in range(2):
        start = side * QUART
        cells = slice(start, start + QUART)
        window = jnp.concatenate(
            [slab[start + i * COL : start + i * COL + QUART] for slab in (low, high) for i in range(3)], axis=1
        )
        value = base[half * HALF + start : half * HALF + start + QUART] + over_height(matmul(window, weights[...]))
        preact[cells] = value
        active = (value * jax.nn.sigmoid(value)).astype(bf16)
        hidden[cells] = active
        sides[side] = matmul(active, proj[...])
    core = core_ref[0]
    keep[...] = sides[core]
    send_0[...] = sides[1 - core, : QUART // 2].astype(bf16)
    send_1[...] = sides[1 - core, QUART // 2 :].astype(bf16)


def prepare_kernel(
    below, centre, above, preact_a, preact_b, hidden_a, hidden_b, slope, hidden_t, features_t
):
    for q in range(4):
        cells = slice(q * QUART, (q + 1) * QUART)
        local = slice(q % 2 * QUART, (q % 2 + 1) * QUART)
        preact, hidden = ((preact_a, hidden_a), (preact_b, hidden_b))[q // 2]
        slope[cells] = silu_slope(preact[local])
        hidden_t[:, cells] = hidden[local].astype(f32).T.astype(bf16)
        for t, slab in enumerate((below, centre, above)):
            value = slab[cells].astype(f32)
            for j, moved in enumerate((from_below(value), value, from_above(value))):
                block = (t * 3 + j) * C
                features_t[block : block + C, cells] = moved.T.astype(bf16)


def d_out_of(summed, cot):
    return (cot.astype(f32) * silu_slope(summed)).astype(bf16)


def head_of(summed):
    return (summed * jax.nn.sigmoid(summed)).astype(bf16)


def first_output_kernel(row_ref, chip_sum, recv, bias, cot_mine, cot_pair, own_0, own_1, head):
    for k, own in enumerate((own_0, own_1)):
        cells = slice(k * (QUART // 2), (k + 1) * (QUART // 2))
        summed = chip_sum[cells] + recv[cells].astype(f32) + bias[...]
        head[cells] = head_of(summed)
        own[...] = d_out_of(summed, jnp.where(row_ref[0] == 0, cot_mine[cells], cot_pair[cells]))


def second_output_kernel(row_ref, chip_sum, recv, bias, cot_mine, cot_pair, head_a, own, head):
    summed = chip_sum[...] + recv[...].astype(f32) + bias[...]
    own[...] = d_out_of(summed, jnp.where(row_ref[0] == 1, cot_mine[...], cot_pair[...]))
    head[...] = jnp.where(row_ref[0] == 0, head_a[...], head_of(summed))


def height_sum(parts):
    return parts[:, 3 * C : 6 * C] + from_above(parts[:, : 3 * C]) + from_below(parts[:, 6 * C :])


def back_rows(core_ref, own, other, slope, proj, d_pre, at, d_out):
    for side in range(2):
        start = side * QUART
        for mine, theirs in zip(own, other):
            count = mine.shape[0]
            rows = jnp.where(core_ref[0] == side, mine[...], theirs[...])
            d_out[start : start + count] = rows
            d_hidden = matmul_rt(rows, proj[...])
            d_pre[at + start : at + start + count] = (d_hidden * slope[start : start + count]).astype(bf16)
            start += count


def back_features(d_pre, weights, start, count):
    window = jnp.concatenate(
        [d_pre[start + (2 - i) * COL : start + (2 - i) * COL + count] for i in range(3)], axis=1
    )
    return height_sum(matmul_rt(window, weights[...]))


def back_first_kernel(
    core_ref, own_0, own_1, other_0, other_1, slope, proj, weights, features_t, hidden_t,
    d_pre, low, mid, high, taps, projs, window, d_out,
):
    d_pre[0:COL] = jnp.zeros((COL, F), bf16)
    back_rows(core_ref, (own_0, own_1), (other_0, other_1), slope, proj, d_pre, COL, d_out)
    for k in range(2):
        step = EARLY // 2
        total = back_features(d_pre, weights, k * step, step)
        cells = slice(k * step, (k + 1) * step)
        low[cells] = total[:, :C].astype(bf16)
        mid[cells] = total[:, C : 2 * C]
        high[cells] = total[:, 2 * C :].astype(bf16)
    for i in range(3):
        window[:, i * F : (i + 1) * F] = d_pre[(2 - i) * COL : (2 - i) * COL + EARLY]
    for t in range(3):
        rows = slice(t * 3 * C, (t + 1) * 3 * C)
        taps[rows] = matmul(features_t[rows, :EARLY], window[...])
    projs[...] = matmul(hidden_t[:, :HALF], d_out[...])


def back_second_kernel(
    core_ref, keep_ref, own, other, slope, proj, weights, features_t, hidden_t,
    d_pre_a, low_a, mid_a, high_a, taps, projs, low, mid, high, grads, d_pre, window, d_out,
):
    d_pre[0 : 5 * COL] = d_pre_a[HALF - 4 * COL :]
    d_pre[5 * COL + HALF :] = jnp.zeros((COL, F), bf16)
    back_rows(core_ref, (own,), (other,), slope.at[HALF:], proj, d_pre, 5 * COL, d_out)
    low[:EARLY] = low_a[...]
    mid[:EARLY] = mid_a[...]
    high[:EARLY] = high_a[...]
    late = ROWS - EARLY
    for k in range(4):
        step = late // 4
        total = back_features(d_pre, weights, k * step, step)
        cells = slice(EARLY + k * step, EARLY + (k + 1) * step)
        low[cells] = total[:, :C].astype(bf16)
        mid[cells] = total[:, C : 2 * C]
        high[cells] = total[:, 2 * C :].astype(bf16)
    for i in range(3):
        window[:, i * F : (i + 1) * F] = d_pre[(2 - i) * COL : (2 - i) * COL + late]
    off_centre = keep_ref[0]
    for t in range(3):
        rows = slice(t * 3 * C, (t + 1) * 3 * C)
        block = taps[rows] + matmul(features_t[rows, EARLY:], window[...])
        for i in range(3):
            for j in range(3):
                tap = (t * 9 + i * 3 + j) * C
                piece = block[j * C : (j + 1) * C, i * F : (i + 1) * F]
                if (t, i, j) != (1, 1, 1):
                    piece = piece * off_centre
                grads[tap : tap + C] = piece.astype(bf16)
    grads[TAPS:] = (projs[...] + matmul(hidden_t[:, HALF:], d_out[...])).astype(bf16)


def core_split_kernel(core_ref, low, mid, high, kept, sent, total):
    for q in range(4):
        cells = slice(q * QUART, (q + 1) * QUART)
        total[q] = mid[cells] + low[cells].astype(f32) + high[cells].astype(f32)
    core = core_ref[0]
    for row in range(2):
        kept[row] = total[2 * row + core]
        sent[row] = total[2 * row + 1 - core].astype(bf16)


def chip_split_kernel(row_ref, kept, recv, mine, sent):
    row = row_ref[0]
    mine[...] = kept[row] + recv[row].astype(f32)
    sent[...] = (kept[1 - row] + recv[1 - row].astype(f32)).astype(bf16)


def sum_of(parts):
    acc = parts[0].astype(f32)
    for k in range(1, parts.shape[0]):
        acc = acc + parts[k].astype(f32)
    return acc.astype(bf16)


def sum_kernel(parts, copies):
    total = sum_of(parts)
    for k in range(copies.shape[0]):
        copies[k] = total


def widen_kernel(total, taps_out, proj_out, wide, sems):
    moves = []
    for k in range(4):
        first = k * TAPS // 4
        last = first + TAPS // 4
        wide[first:last] = total[first:last].astype(f32)
        moves.append(pltpu.make_async_copy(wide.at[first:last], taps_out.at[first:last], sems.at[k]))
        moves[-1].start()
    wide[TAPS:] = total[TAPS:].astype(f32)
    moves.append(pltpu.make_async_copy(wide.at[TAPS:], proj_out, sems.at[4]))
    moves[-1].start()
    for move in moves:
        move.wait()


def call(kernel, outs, specs, scratch, flops, *args, place=VMEM):
    return pl.pallas_call(
        kernel,
        out_shape=[jax.ShapeDtypeStruct(*o) for o in outs],
        in_specs=specs,
        out_specs=[place] * len(outs),
        scratch_shapes=scratch,
        compiler_params=pltpu.CompilerParams(vmem_limit_bytes=12 * 1024 * 1024),
        cost_estimate=pl.CostEstimate(flops=flops, bytes_accessed=flops // 1000, transcendentals=0),
    )(*args)


def depth_pairs(mesh_gz, sign):
    strides = (0, 1, 2, 4)
    pairs = []
    for g in range(mesh_gz):
        for b in range(1, 4):
            target = g + sign * strides[b]
            if 0 <= target < mesh_gz:
                pairs.append((g * 4 + b, target * 4 + b))
    return pairs


def exchanged(parts, axis):
    return jnp.concatenate([lax.ppermute(part, axis, SWAP) for part in parts], axis=0).astype(f32)


def shards(slabs, features, tap_weights, branch_bias, proj_weights, out_bias, cotangent):
    branch = lax.axis_index(BR)
    core = lax.axis_index("c")
    row = lax.axis_index("yl")
    core_arg = core.astype(jnp.int32)[None]
    row_arg = row.astype(jnp.int32)[None]
    up = depth_pairs(slabs, 1)
    down = depth_pairs(slabs, -1)
    everywhere = GZ + BR
    proj = proj_weights[0]

    centre = lax.all_gather(features.reshape(QUART, C), BR, axis=0, tiled=True)
    tap = jnp.arange(27).reshape(3, 3, 3)
    off_centre = jnp.where(branch > 0, 1.0, 0.0).astype(f32)
    mask = jnp.where(tap == 13, 1.0, off_centre).astype(bf16)
    cot_mine = cotangent.reshape(QUART, F)
    centre, cot_mine = lax.optimization_barrier((centre, cot_mine))
    below = lax.ppermute(centre, everywhere, up)
    above = lax.ppermute(centre, everywhere, down)
    cot_pair = lax.ppermute(cot_mine, "yl", SWAP)
    masked = tap_weights[0] * mask[:, :, :, None, None]
    by_window = masked.transpose(0, 1, 3, 2, 4).reshape(3, 3 * C, 3 * F)
    weights_mid = by_window[1]
    weights_out = jnp.concatenate([by_window[0], by_window[2]], axis=0)
    weights_bwd = masked.transpose(2, 0, 3, 1, 4).reshape(9 * C, 3 * F)
    (base,) = call(
        centre_kernel,
        [((ROWS, F), f32)],
        [VMEM] * 3,
        [pltpu.VMEM((ROWS + 2 * COL, C), bf16)],
        2 * ROWS * 9 * C * F,
        centre, weights_mid, branch_bias,
    )
    below, above, cot_pair, base, weights_out, weights_bwd = lax.optimization_barrier(
        (below, above, cot_pair, base, weights_out, weights_bwd)
    )

    def forward_half(half, base):
        return call(
            functools.partial(forward_kernel, half),
            [((HALF, F), f32), ((HALF, F), bf16), ((QUART, F), f32)] + [((QUART // 2, F), bf16)] * 2,
            [SMEM] + [VMEM] * 5,
            [pltpu.VMEM((HALF + 2 * COL, C), bf16)] * 2 + [pltpu.VMEM((2, QUART, F), f32)],
            1000,
            core_arg, below, above, weights_out, base, proj,
        )

    preact_a, hidden_a, keep_a, *send_a = forward_half(0, base)
    chip_a = keep_a + exchanged(send_a, "c")
    preact_b, hidden_b, keep_b, *send_b = forward_half(1, base)
    chip_send_a, *send_b = lax.optimization_barrier((chip_a.astype(bf16), *send_b))
    recv_a = lax.ppermute(chip_send_a, "yl", SWAP)
    chip_b = keep_b + exchanged(send_b, "c")
    chip_send_b, preact_b = lax.optimization_barrier((chip_b.astype(bf16), preact_b))
    recv_b = lax.ppermute(chip_send_b, "yl", SWAP)
    slope, hidden_t, features_t = call(
        prepare_kernel,
        [((ROWS, F), f32), ((F, ROWS), bf16), ((9 * C, ROWS), bf16)],
        [VMEM] * 7,
        [],
        1000,
        below, centre, above, preact_a, preact_b, hidden_a, hidden_b,
    )
    recv_a, slope, hidden_t, features_t = lax.optimization_barrier((recv_a, slope, hidden_t, features_t))

    *own_a, head_a = call(
        first_output_kernel,
        [((QUART // 2, F), bf16), ((QUART // 2, F), bf16), ((QUART, F), bf16)],
        [SMEM] + [VMEM] * 5,
        [],
        1000,
        row_arg, chip_a, recv_a, out_bias[None], cot_mine, cot_pair,
    )
    other_a = [lax.ppermute(part, "c", SWAP) for part in own_a]
    d_pre_a, low_a, mid_a, high_a, taps_a, projs_a = call(
        back_first_kernel,
        [
            ((HALF + COL, F), bf16),
            ((EARLY, C), bf16),
            ((EARLY, C), f32),
            ((EARLY, C), bf16),
            ((9 * C, 3 * F), f32),
            ((F, F), f32),
        ],
        [SMEM] + [VMEM] * 9,
        [pltpu.VMEM((EARLY, 3 * F), bf16), pltpu.VMEM((HALF, F), bf16)],
        1000,
        core_arg, *own_a, *other_a, slope, proj, weights_bwd, features_t, hidden_t,
    )
    recv_b, taps_a, d_pre_a = lax.optimization_barrier((recv_b, taps_a, d_pre_a))
    own_b, head_out = call(
        second_output_kernel,
        [((QUART, F), bf16), ((QUART, F), bf16)],
        [SMEM] + [VMEM] * 6,
        [],
        1000,
        row_arg, chip_b, recv_b, out_bias[None], cot_mine, cot_pair, head_a,
    )
    other_b = lax.ppermute(own_b, "c", SWAP)
    low, mid, high, grads = call(
        back_second_kernel,
        [((ROWS, C), bf16), ((ROWS, C), f32), ((ROWS, C), bf16), ((GRAD_ROWS, F), bf16)],
        [SMEM, SMEM] + [VMEM] * 13,
        [
            pltpu.VMEM((HALF + 6 * COL, F), bf16),
            pltpu.VMEM((ROWS - EARLY, 3 * F), bf16),
            pltpu.VMEM((HALF, F), bf16),
        ],
        2 * ROWS * 27 * C * F,
        core_arg, off_centre[None], own_b, other_b, slope, proj, weights_bwd, features_t, hidden_t,
        d_pre_a, low_a, mid_a, high_a, taps_a, projs_a,
    )
    near = math.prod(lax.axis_size(a) for a in NEAR)
    far = lax.axis_size(FAR)
    share = GRAD_ROWS // near
    grads, low, mid, high = lax.optimization_barrier((grads, low, mid, high))
    part = lax.all_to_all(grads.reshape(near, share, F), NEAR, 0, 0, tiled=True)
    part, low, mid, high = lax.optimization_barrier((part, low, mid, high))

    def sum_for(peers, parts):
        return call(
            sum_kernel,
            [((peers, share, F), bf16)],
            [VMEM],
            [],
            1_000_000,
            parts,
        )[0]

    part = sum_for(far, part)
    part, low, high = lax.optimization_barrier((part, low, high))
    from_low = lax.ppermute(low, everywhere, down)
    from_high = lax.ppermute(high, everywhere, up)
    part = lax.all_to_all(part, FAR, 0, 0, tiled=True)
    part = sum_for(near, part)

    kept, sent = call(
        core_split_kernel,
        [((2, QUART, C), f32), ((2, QUART, C), bf16)],
        [SMEM] + [VMEM] * 3,
        [pltpu.VMEM((4, QUART, C), f32)],
        1_000_000,
        core_arg, from_low, mid, from_high,
    )
    mine, sent = call(
        chip_split_kernel,
        [((QUART, C), f32), ((QUART, C), bf16)],
        [SMEM] + [VMEM] * 2,
        [],
        1_000_000,
        row_arg, kept, lax.ppermute(sent, "c", SWAP),
    )
    recv = lax.ppermute(sent, "yl", SWAP)
    feature_grad = (mine + recv.astype(f32)).astype(bf16)
    part, feature_grad = lax.optimization_barrier((part, feature_grad))
    total = lax.all_to_all(part, NEAR, 0, 0, tiled=True).reshape(GRAD_ROWS, F)
    taps, proj_total = call(
        widen_kernel,
        [((TAPS, F), f32), ((F, F), f32)],
        [VMEM],
        [pltpu.VMEM((GRAD_ROWS, F), f32), pltpu.SemaphoreType.DMA((5,))],
        1_000_000,
        total,
        place=HBM,
    )
    return (
        head_out.reshape(cotangent.shape),
        feature_grad.reshape(features.shape),
        taps.reshape(1, 3, 3, 3, C, F),
        proj_total.reshape(1, F, F),
    )


def solution(mesh):
    slabs = mesh.shape["gz"]
    split = (4, 2, 4, 2) if slabs == 64 else (slabs, 1, 1, 1)
    fine = Mesh(mesh.devices.reshape(split + (2, 2)), GZ + BR)
    in_specs = (
        P(BR, GZ, None, None),
        P(BR, None, None, None, None, None),
        P(BR, None),
        P(BR, None, None),
        P(),
        P(BR, GZ, None, None),
    )
    out_specs = (
        P(BR, GZ, None, None),
        P(BR, GZ, None, None),
        P(BR, None, None, None, None, None),
        P(BR, None, None),
    )
    return jax.shard_map(
        functools.partial(shards, slabs), mesh=fine, in_specs=in_specs, out_specs=out_specs, check_vma=False
    )
```

```python
import functools
import math

import jax
import jax.numpy as jnp
from jax import lax
from jax.experimental import pallas as pl
from jax.experimental.pallas import tpu as pltpu
from jax.sharding import Mesh
from jax.sharding import PartitionSpec as P

C = 128
F = 256
COL = 64
ROWS = 2048
HALF = 1024
EARLY = 12 * COL
QUART = 512
TAPS = 27 * C
GRAD_ROWS = TAPS + F
bf16 = jnp.bfloat16
f32 = jnp.float32
GZ = ("zh", "zl", "x", "yh")
NEAR = ("zl", "x", "yh")
FAR = "zh"
BR = ("yl", "c")
SWAP = [(0, 1), (1, 0)]
VMEM = pl.BlockSpec(memory_space=pltpu.VMEM)
HBM = pl.BlockSpec(memory_space=pltpu.HBM)
SMEM = pl.BlockSpec(memory_space=pltpu.SMEM)


def silu_slope(values):
    logistic = jax.nn.sigmoid(values)
    return logistic * (1.0 + values * (1.0 - logistic))


def height_of(rows, lanes):
    return lax.broadcasted_iota(jnp.int32, (rows, lanes), 0) & 15


def from_below(values):
    rolled = pltpu.roll(values, 1, 0)
    return jnp.where(height_of(*values.shape) == 0, 0.0, rolled)


def from_above(values):
    rolled = pltpu.roll(values, values.shape[0] - 1, 0)
    return jnp.where(height_of(*values.shape) == 15, 0.0, rolled)


def matmul(lhs, rhs):
    return jnp.dot(lhs, rhs, preferred_element_type=f32)


def matmul_rt(lhs, rhs):
    return lax.dot_general(lhs, rhs, (((1,), (1,)), ((), ())), preferred_element_type=f32)


def pad_columns(padded, slab):
    padded[0:COL] = jnp.zeros((COL, C), bf16)
    padded[COL + ROWS : 2 * COL + ROWS] = jnp.zeros((COL, C), bf16)
    padded[COL : COL + ROWS] = slab[...]


def pad_half(padded, slab, half):
    if half == 0:
        padded[0:COL] = jnp.zeros((COL, C), bf16)
        padded[COL:] = slab[0 : HALF + COL]
    else:
        padded[0 : HALF + COL] = slab[HALF - COL :]
        padded[HALF + COL :] = jnp.zeros((COL, C), bf16)


def over_height(parts):
    return parts[:, F : 2 * F] + from_below(parts[:, :F]) + from_above(parts[:, 2 * F :])


def centre_kernel(centre, weights, bias, base, padded):
    pad_columns(padded, centre)
    for q in range(4):
        start = q * QUART
        window = jnp.concatenate([padded[start + i * COL : start + i * COL + QUART] for i in range(3)], axis=1)
        base[start : start + QUART] = bias[...] + over_height(matmul(window, weights[...]))


def forward_kernel(
    half, core_ref, below, above, weights, base, proj, preact, hidden, keep, send_0, send_1, low, high, sides
):
    pad_half(low, below, half)
    pad_half(high, above, half)
    for side in range(2):
        start = side * QUART
        cells = slice(start, start + QUART)
        window = jnp.concatenate(
            [slab[start + i * COL : start + i * COL + QUART] for slab in (low, high) for i in range(3)], axis=1
        )
        value = base[half * HALF + start : half * HALF + start + QUART] + over_height(matmul(window, weights[...]))
        preact[cells] = value
        active = (value * jax.nn.sigmoid(value)).astype(bf16)
        hidden[cells] = active
        sides[side] = matmul(active, proj[...])
    core = core_ref[0]
    keep[...] = sides[core]
    send_0[...] = sides[1 - core, : QUART // 2].astype(bf16)
    send_1[...] = sides[1 - core, QUART // 2 :].astype(bf16)


def prepare_kernel(
    below, centre, above, preact_a, preact_b, hidden_a, hidden_b, slope, hidden_t, features_t
):
    for q in range(4):
        cells = slice(q * QUART, (q + 1) * QUART)
        local = slice(q % 2 * QUART, (q % 2 + 1) * QUART)
        preact, hidden = ((preact_a, hidden_a), (preact_b, hidden_b))[q // 2]
        slope[cells] = silu_slope(preact[local])
        hidden_t[:, cells] = hidden[local].astype(f32).T.astype(bf16)
        for t, slab in enumerate((below, centre, above)):
            value = slab[cells].astype(f32)
            for j, moved in enumerate((from_below(value), value, from_above(value))):
                block = (t * 3 + j) * C
                features_t[block : block + C, cells] = moved.T.astype(bf16)


def d_out_of(summed, cot):
    return (cot.astype(f32) * silu_slope(summed)).astype(bf16)


def head_of(summed):
    return (summed * jax.nn.sigmoid(summed)).astype(bf16)


def first_output_kernel(row_ref, chip_sum, recv, bias, cot_mine, cot_pair, own_0, own_1, head):
    for k, own in enumerate((own_0, own_1)):
        cells = slice(k * (QUART // 2), (k + 1) * (QUART // 2))
        summed = chip_sum[cells] + recv[cells].astype(f32) + bias[...]
        head[cells] = head_of(summed)
        own[...] = d_out_of(summed, jnp.where(row_ref[0] == 0, cot_mine[cells], cot_pair[cells]))


def second_output_kernel(row_ref, chip_sum, recv, bias, cot_mine, cot_pair, head_a, own, head):
    summed = chip_sum[...] + recv[...].astype(f32) + bias[...]
    own[...] = d_out_of(summed, jnp.where(row_ref[0] == 1, cot_mine[...], cot_pair[...]))
    head[...] = jnp.where(row_ref[0] == 0, head_a[...], head_of(summed))


def height_sum(parts):
    return parts[:, 3 * C : 6 * C] + from_above(parts[:, : 3 * C]) + from_below(parts[:, 6 * C :])


def back_rows(core_ref, own, other, slope, proj, d_pre, at, d_out):
    for side in range(2):
        start = side * QUART
        for mine, theirs in zip(own, other):
            count = mine.shape[0]
            rows = jnp.where(core_ref[0] == side, mine[...], theirs[...])
            d_out[start : start + count] = rows
            d_hidden = matmul_rt(rows, proj[...])
            d_pre[at + start : at + start + count] = (d_hidden * slope[start : start + count]).astype(bf16)
            start += count


def back_features(d_pre, weights, start, count):
    window = jnp.concatenate(
        [d_pre[start + (2 - i) * COL : start + (2 - i) * COL + count] for i in range(3)], axis=1
    )
    return height_sum(matmul_rt(window, weights[...]))


def back_first_kernel(
    core_ref, own_0, own_1, other_0, other_1, slope, proj, weights, features_t, hidden_t,
    d_pre, low, mid, high, taps, projs, window, d_out,
):
    d_pre[0:COL] = jnp.zeros((COL, F), bf16)
    back_rows(core_ref, (own_0, own_1), (other_0, other_1), slope, proj, d_pre, COL, d_out)
    for k in range(2):
        step = EARLY // 2
        total = back_features(d_pre, weights, k * step, step)
        cells = slice(k * step, (k + 1) * step)
        low[cells] = total[:, :C].astype(bf16)
        mid[cells] = total[:, C : 2 * C]
        high[cells] = total[:, 2 * C :].astype(bf16)
    for i in range(3):
        window[:, i * F : (i + 1) * F] = d_pre[(2 - i) * COL : (2 - i) * COL + EARLY]
    for t in range(3):
        rows = slice(t * 3 * C, (t + 1) * 3 * C)
        taps[rows] = matmul(features_t[rows, :EARLY], window[...])
    projs[...] = matmul(hidden_t[:, :HALF], d_out[...])


def back_second_kernel(
    core_ref, keep_ref, own, other, slope, proj, weights, features_t, hidden_t,
    d_pre_a, low_a, mid_a, high_a, taps, projs, low_out, mid, high, grads, d_pre, window, d_out, low, sem,
):
    d_pre[0 : 5 * COL] = d_pre_a[HALF - 4 * COL :]
    d_pre[5 * COL + HALF :] = jnp.zeros((COL, F), bf16)
    back_rows(core_ref, (own,), (other,), slope.at[HALF:], proj, d_pre, 5 * COL, d_out)
    low[:EARLY] = low_a[...]
    mid[:EARLY] = mid_a[...]
    high[:EARLY] = high_a[...]
    late = ROWS - EARLY
    for k in range(4):
        step = late // 4
        total = back_features(d_pre, weights, k * step, step)
        cells = slice(EARLY + k * step, EARLY + (k + 1) * step)
        low[cells] = total[:, :C].astype(bf16)
        mid[cells] = total[:, C : 2 * C]
        high[cells] = total[:, 2 * C :].astype(bf16)
    low_copy = pltpu.make_async_copy(low, low_out, sem)
    low_copy.start()
    for i in range(3):
        window[:, i * F : (i + 1) * F] = d_pre[(2 - i) * COL : (2 - i) * COL + late]
    off_centre = keep_ref[0]
    for t in range(3):
        rows = slice(t * 3 * C, (t + 1) * 3 * C)
        block = taps[rows] + matmul(features_t[rows, EARLY:], window[...])
        for i in range(3):
            for j in range(3):
                tap = (t * 9 + i * 3 + j) * C
                piece = block[j * C : (j + 1) * C, i * F : (i + 1) * F]
                if (t, i, j) != (1, 1, 1):
                    piece = piece * off_centre
                grads[tap : tap + C] = piece.astype(bf16)
    grads[TAPS:] = (projs[...] + matmul(hidden_t[:, HALF:], d_out[...])).astype(bf16)
    low_copy.wait()


def core_split_kernel(core_ref, low, mid, high, kept, sent, total):
    for q in range(4):
        cells = slice(q * QUART, (q + 1) * QUART)
        total[q] = mid[cells] + low[cells].astype(f32) + high[cells].astype(f32)
    core = core_ref[0]
    for row in range(2):
        kept[row] = total[2 * row + core]
        sent[row] = total[2 * row + 1 - core].astype(bf16)


def chip_split_kernel(row_ref, kept, recv, mine, sent):
    row = row_ref[0]
    mine[...] = kept[row] + recv[row].astype(f32)
    sent[...] = (kept[1 - row] + recv[1 - row].astype(f32)).astype(bf16)


def sum_of(parts):
    acc = parts[0].astype(f32)
    for k in range(1, parts.shape[0]):
        acc = acc + parts[k].astype(f32)
    return acc.astype(bf16)


def sum_kernel(parts, copies):
    total = sum_of(parts)
    for k in range(copies.shape[0]):
        copies[k] = total


def widen_kernel(total, taps_out, proj_out, wide, sems):
    moves = []
    for k in range(4):
        first = k * TAPS // 4
        last = first + TAPS // 4
        wide[first:last] = total[first:last].astype(f32)
        moves.append(pltpu.make_async_copy(wide.at[first:last], taps_out.at[first:last], sems.at[k]))
        moves[-1].start()
    wide[TAPS:] = total[TAPS:].astype(f32)
    moves.append(pltpu.make_async_copy(wide.at[TAPS:], proj_out, sems.at[4]))
    moves[-1].start()
    for move in moves:
        move.wait()


def call(kernel, outs, specs, scratch, flops, *args, place=VMEM):
    return pl.pallas_call(
        kernel,
        out_shape=[jax.ShapeDtypeStruct(*o) for o in outs],
        in_specs=specs,
        out_specs=place if isinstance(place, list) else [place] * len(outs),
        scratch_shapes=scratch,
        compiler_params=pltpu.CompilerParams(vmem_limit_bytes=12 * 1024 * 1024),
        cost_estimate=pl.CostEstimate(flops=flops, bytes_accessed=flops // 1000, transcendentals=0),
    )(*args)


def depth_pairs(mesh_gz, sign):
    strides = (0, 1, 2, 4)
    pairs = []
    for g in range(mesh_gz):
        for b in range(1, 4):
            target = g + sign * strides[b]
            if 0 <= target < mesh_gz:
                pairs.append((g * 4 + b, target * 4 + b))
    return pairs


def exchanged(parts, axis):
    return jnp.concatenate([lax.ppermute(part, axis, SWAP) for part in parts], axis=0).astype(f32)


def shards(slabs, features, tap_weights, branch_bias, proj_weights, out_bias, cotangent):
    branch = lax.axis_index(BR)
    core = lax.axis_index("c")
    row = lax.axis_index("yl")
    core_arg = core.astype(jnp.int32)[None]
    row_arg = row.astype(jnp.int32)[None]
    up = depth_pairs(slabs, 1)
    down = depth_pairs(slabs, -1)
    everywhere = GZ + BR
    proj = proj_weights[0]

    centre = lax.all_gather(features.reshape(QUART, C), BR, axis=0, tiled=True)
    tap = jnp.arange(27).reshape(3, 3, 3)
    off_centre = jnp.where(branch > 0, 1.0, 0.0).astype(f32)
    mask = jnp.where(tap == 13, 1.0, off_centre).astype(bf16)
    cot_mine = cotangent.reshape(QUART, F)
    centre, cot_mine = lax.optimization_barrier((centre, cot_mine))
    below = lax.ppermute(centre, everywhere, up)
    above = lax.ppermute(centre, everywhere, down)
    cot_pair = lax.ppermute(cot_mine, "yl", SWAP)
    masked = tap_weights[0] * mask[:, :, :, None, None]
    by_window = masked.transpose(0, 1, 3, 2, 4).reshape(3, 3 * C, 3 * F)
    weights_mid = by_window[1]
    weights_out = jnp.concatenate([by_window[0], by_window[2]], axis=0)
    weights_bwd = masked.transpose(2, 0, 3, 1, 4).reshape(9 * C, 3 * F)
    (base,) = call(
        centre_kernel,
        [((ROWS, F), f32)],
        [VMEM] * 3,
        [pltpu.VMEM((ROWS + 2 * COL, C), bf16)],
        2 * ROWS * 9 * C * F,
        centre, weights_mid, branch_bias,
    )
    below, above, cot_pair, base, weights_out, weights_bwd = lax.optimization_barrier(
        (below, above, cot_pair, base, weights_out, weights_bwd)
    )

    def forward_half(half, base):
        return call(
            functools.partial(forward_kernel, half),
            [((HALF, F), f32), ((HALF, F), bf16), ((QUART, F), f32)] + [((QUART // 2, F), bf16)] * 2,
            [SMEM] + [VMEM] * 5,
            [pltpu.VMEM((HALF + 2 * COL, C), bf16)] * 2 + [pltpu.VMEM((2, QUART, F), f32)],
            1000,
            core_arg, below, above, weights_out, base, proj,
        )

    preact_a, hidden_a, keep_a, *send_a = forward_half(0, base)
    chip_a = keep_a + exchanged(send_a, "c")
    preact_b, hidden_b, keep_b, *send_b = forward_half(1, base)
    chip_send_a, *send_b = lax.optimization_barrier((chip_a.astype(bf16), *send_b))
    recv_a = lax.ppermute(chip_send_a, "yl", SWAP)
    chip_b = keep_b + exchanged(send_b, "c")
    chip_send_b, preact_b = lax.optimization_barrier((chip_b.astype(bf16), preact_b))
    recv_b = lax.ppermute(chip_send_b, "yl", SWAP)
    slope, hidden_t, features_t = call(
        prepare_kernel,
        [((ROWS, F), f32), ((F, ROWS), bf16), ((9 * C, ROWS), bf16)],
        [VMEM] * 7,
        [],
        1000,
        below, centre, above, preact_a, preact_b, hidden_a, hidden_b,
    )
    recv_a, slope, hidden_t, features_t = lax.optimization_barrier((recv_a, slope, hidden_t, features_t))

    *own_a, head_a = call(
        first_output_kernel,
        [((QUART // 2, F), bf16), ((QUART // 2, F), bf16), ((QUART, F), bf16)],
        [SMEM] + [VMEM] * 5,
        [],
        1000,
        row_arg, chip_a, recv_a, out_bias[None], cot_mine, cot_pair,
    )
    other_a = [lax.ppermute(part, "c", SWAP) for part in own_a]
    d_pre_a, low_a, mid_a, high_a, taps_a, projs_a = call(
        back_first_kernel,
        [
            ((HALF + COL, F), bf16),
            ((EARLY, C), bf16),
            ((EARLY, C), f32),
            ((EARLY, C), bf16),
            ((9 * C, 3 * F), f32),
            ((F, F), f32),
        ],
        [SMEM] + [VMEM] * 9,
        [pltpu.VMEM((EARLY, 3 * F), bf16), pltpu.VMEM((HALF, F), bf16)],
        1000,
        core_arg, *own_a, *other_a, slope, proj, weights_bwd, features_t, hidden_t,
    )
    recv_b, taps_a, d_pre_a = lax.optimization_barrier((recv_b, taps_a, d_pre_a))
    own_b, head_out = call(
        second_output_kernel,
        [((QUART, F), bf16), ((QUART, F), bf16)],
        [SMEM] + [VMEM] * 6,
        [],
        1000,
        row_arg, chip_b, recv_b, out_bias[None], cot_mine, cot_pair, head_a,
    )
    other_b = lax.ppermute(own_b, "c", SWAP)
    low, mid, high, grads = call(
        back_second_kernel,
        [((ROWS, C), bf16), ((ROWS, C), f32), ((ROWS, C), bf16), ((GRAD_ROWS, F), bf16)],
        [SMEM, SMEM] + [VMEM] * 13,
        [
            pltpu.VMEM((HALF + 6 * COL, F), bf16),
            pltpu.VMEM((ROWS - EARLY, 3 * F), bf16),
            pltpu.VMEM((HALF, F), bf16),
            pltpu.VMEM((ROWS, C), bf16),
            pltpu.SemaphoreType.DMA(()),
        ],
        2 * ROWS * 27 * C * F,
        core_arg, off_centre[None], own_b, other_b, slope, proj, weights_bwd, features_t, hidden_t,
        d_pre_a, low_a, mid_a, high_a, taps_a, projs_a,
        place=[HBM, VMEM, VMEM, VMEM],
    )
    near = math.prod(lax.axis_size(a) for a in NEAR)
    far = lax.axis_size(FAR)
    share = GRAD_ROWS // near
    grads, low, mid, high = lax.optimization_barrier((grads, low, mid, high))
    part = lax.all_to_all(grads.reshape(near, share, F), NEAR, 0, 0, tiled=True)
    part, low, mid, high = lax.optimization_barrier((part, low, mid, high))

    def sum_for(peers, parts):
        return call(
            sum_kernel,
            [((peers, share, F), bf16)],
            [VMEM],
            [],
            1_000_000,
            parts,
        )[0]

    part = sum_for(far, part)
    from_low = lax.ppermute(low, everywhere, down)
    from_high = lax.ppermute(high, everywhere, up)
    part = lax.all_to_all(part, FAR, 0, 0, tiled=True)
    part = sum_for(near, part)

    kept, sent = call(
        core_split_kernel,
        [((2, QUART, C), f32), ((2, QUART, C), bf16)],
        [SMEM] + [VMEM] * 3,
        [pltpu.VMEM((4, QUART, C), f32)],
        1_000_000,
        core_arg, from_low, mid, from_high,
    )
    mine, sent = call(
        chip_split_kernel,
        [((QUART, C), f32), ((QUART, C), bf16)],
        [SMEM] + [VMEM] * 2,
        [],
        1_000_000,
        row_arg, kept, lax.ppermute(sent, "c", SWAP),
    )
    recv = lax.ppermute(sent, "yl", SWAP)
    feature_grad = (mine + recv.astype(f32)).astype(bf16)
    part, feature_grad = lax.optimization_barrier((part, feature_grad))
    total = lax.all_to_all(part, NEAR, 0, 0, tiled=True).reshape(GRAD_ROWS, F)
    taps, proj_total = call(
        widen_kernel,
        [((TAPS, F), f32), ((F, F), f32)],
        [VMEM],
        [pltpu.VMEM((GRAD_ROWS, F), f32), pltpu.SemaphoreType.DMA((5,))],
        1_000_000,
        total,
        place=HBM,
    )
    return (
        head_out.reshape(cotangent.shape),
        feature_grad.reshape(features.shape),
        taps.reshape(1, 3, 3, 3, C, F),
        proj_total.reshape(1, F, F),
    )


def solution(mesh):
    slabs = mesh.shape["gz"]
    split = (4, 2, 4, 2) if slabs == 64 else (slabs, 1, 1, 1)
    fine = Mesh(mesh.devices.reshape(split + (2, 2)), GZ + BR)
    in_specs = (
        P(BR, GZ, None, None),
        P(BR, None, None, None, None, None),
        P(BR, None),
        P(BR, None, None),
        P(),
        P(BR, GZ, None, None),
    )
    out_specs = (
        P(BR, GZ, None, None),
        P(BR, GZ, None, None),
        P(BR, None, None, None, None, None),
        P(BR, None, None),
    )
    return jax.shard_map(
        functools.partial(shards, slabs), mesh=fine, in_specs=in_specs, out_specs=out_specs, check_vma=False
    )
```

```python
import functools
import math

import jax
import jax.numpy as jnp
from jax import lax
from jax.experimental import pallas as pl
from jax.experimental.pallas import tpu as pltpu
from jax.sharding import Mesh
from jax.sharding import PartitionSpec as P

C = 128
F = 256
COL = 64
ROWS = 2048
HALF = 1024
EARLY = 12 * COL
QUART = 512
TAPS = 27 * C
GRAD_ROWS = TAPS + F
bf16 = jnp.bfloat16
f32 = jnp.float32
GZ = ("zh", "zl", "x", "yh")
NEAR = ("zl", "x", "yh")
FAR = "zh"
BR = ("yl", "c")
SWAP = [(0, 1), (1, 0)]
VMEM = pl.BlockSpec(memory_space=pltpu.VMEM)
HBM = pl.BlockSpec(memory_space=pltpu.HBM)
SMEM = pl.BlockSpec(memory_space=pltpu.SMEM)


def silu_slope(values):
    logistic = jax.nn.sigmoid(values)
    return logistic * (1.0 + values * (1.0 - logistic))


def height_of(rows, lanes):
    return lax.broadcasted_iota(jnp.int32, (rows, lanes), 0) & 15


def from_below(values):
    rolled = pltpu.roll(values, 1, 0)
    return jnp.where(height_of(*values.shape) == 0, 0.0, rolled)


def from_above(values):
    rolled = pltpu.roll(values, values.shape[0] - 1, 0)
    return jnp.where(height_of(*values.shape) == 15, 0.0, rolled)


def matmul(lhs, rhs):
    return jnp.dot(lhs, rhs, preferred_element_type=f32)


def matmul_rt(lhs, rhs):
    return lax.dot_general(lhs, rhs, (((1,), (1,)), ((), ())), preferred_element_type=f32)


def pad_columns(padded, slab):
    padded[0:COL] = jnp.zeros((COL, C), bf16)
    padded[COL + ROWS : 2 * COL + ROWS] = jnp.zeros((COL, C), bf16)
    padded[COL : COL + ROWS] = slab[...]


def pad_half(padded, slab, half):
    if half == 0:
        padded[0:COL] = jnp.zeros((COL, C), bf16)
        padded[COL:] = slab[0 : HALF + COL]
    else:
        padded[0 : HALF + COL] = slab[HALF - COL :]
        padded[HALF + COL :] = jnp.zeros((COL, C), bf16)


def over_height(parts):
    return parts[:, F : 2 * F] + from_below(parts[:, :F]) + from_above(parts[:, 2 * F :])


def centre_kernel(centre, weights, bias, base, padded):
    pad_columns(padded, centre)
    for q in range(4):
        start = q * QUART
        window = jnp.concatenate([padded[start + i * COL : start + i * COL + QUART] for i in range(3)], axis=1)
        base[start : start + QUART] = bias[...] + over_height(matmul(window, weights[...]))


def forward_kernel(
    half, core_ref, below, above, weights, base, proj, preact, hidden, keep, send_0, send_1, low, high, sides
):
    pad_half(low, below, half)
    pad_half(high, above, half)
    for side in range(2):
        start = side * QUART
        cells = slice(start, start + QUART)
        window = jnp.concatenate(
            [slab[start + i * COL : start + i * COL + QUART] for slab in (low, high) for i in range(3)], axis=1
        )
        value = base[half * HALF + start : half * HALF + start + QUART] + over_height(matmul(window, weights[...]))
        preact[cells] = value
        active = (value * jax.nn.sigmoid(value)).astype(bf16)
        hidden[cells] = active
        sides[side] = matmul(active, proj[...])
    core = core_ref[0]
    keep[...] = sides[core]
    send_0[...] = sides[1 - core, : QUART // 2].astype(bf16)
    send_1[...] = sides[1 - core, QUART // 2 :].astype(bf16)


def prepare_kernel(
    below, centre, above, preact_a, preact_b, hidden_a, hidden_b, slope, hidden_t, features_t
):
    for q in range(4):
        cells = slice(q * QUART, (q + 1) * QUART)
        local = slice(q % 2 * QUART, (q % 2 + 1) * QUART)
        preact, hidden = ((preact_a, hidden_a), (preact_b, hidden_b))[q // 2]
        slope[cells] = silu_slope(preact[local])
        hidden_t[:, cells] = hidden[local].astype(f32).T.astype(bf16)
        for t, slab in enumerate((below, centre, above)):
            value = slab[cells].astype(f32)
            for j, moved in enumerate((from_below(value), value, from_above(value))):
                block = (t * 3 + j) * C
                features_t[block : block + C, cells] = moved.T.astype(bf16)


def d_out_of(summed, cot):
    return (cot.astype(f32) * silu_slope(summed)).astype(bf16)


def head_of(summed):
    return (summed * jax.nn.sigmoid(summed)).astype(bf16)


def first_output_kernel(row_ref, chip_sum, recv, bias, cot_mine, cot_pair, own_0, own_1):
    for k, own in enumerate((own_0, own_1)):
        cells = slice(k * (QUART // 2), (k + 1) * (QUART // 2))
        summed = chip_sum[cells] + recv[cells].astype(f32) + bias[...]
        own[...] = d_out_of(summed, jnp.where(row_ref[0] == 0, cot_mine[cells], cot_pair[cells]))


def second_output_kernel(row_ref, chip_sum, recv, bias, cot_mine, cot_pair, own):
    summed = chip_sum[...] + recv[...].astype(f32) + bias[...]
    own[...] = d_out_of(summed, jnp.where(row_ref[0] == 1, cot_mine[...], cot_pair[...]))


def first_head_kernel(chip_sum, recv, bias, head):
    head[...] = head_of(chip_sum[...] + recv[...].astype(f32) + bias[...])


def second_head_kernel(row_ref, chip_sum, recv, bias, head_a, head):
    summed = chip_sum[...] + recv[...].astype(f32) + bias[...]
    head[...] = jnp.where(row_ref[0] == 0, head_a[...], head_of(summed))


def height_sum(parts):
    return parts[:, 3 * C : 6 * C] + from_above(parts[:, : 3 * C]) + from_below(parts[:, 6 * C :])


def back_rows(core_ref, own, other, slope, proj, d_pre, at, d_out):
    for side in range(2):
        start = side * QUART
        for mine, theirs in zip(own, other):
            count = mine.shape[0]
            rows = jnp.where(core_ref[0] == side, mine[...], theirs[...])
            d_out[start : start + count] = rows
            d_hidden = matmul_rt(rows, proj[...])
            d_pre[at + start : at + start + count] = (d_hidden * slope[start : start + count]).astype(bf16)
            start += count


def back_features(d_pre, weights, start, count):
    window = jnp.concatenate(
        [d_pre[start + (2 - i) * COL : start + (2 - i) * COL + count] for i in range(3)], axis=1
    )
    return height_sum(matmul_rt(window, weights[...]))


def back_first_kernel(
    core_ref, own_0, own_1, other_0, other_1, slope, proj, weights, features_t, hidden_t,
    d_pre, low, mid, high, taps, projs, window, d_out,
):
    d_pre[0:COL] = jnp.zeros((COL, F), bf16)
    back_rows(core_ref, (own_0, own_1), (other_0, other_1), slope, proj, d_pre, COL, d_out)
    for k in range(2):
        step = EARLY // 2
        total = back_features(d_pre, weights, k * step, step)
        cells = slice(k * step, (k + 1) * step)
        low[cells] = total[:, :C].astype(bf16)
        mid[cells] = total[:, C : 2 * C]
        high[cells] = total[:, 2 * C :].astype(bf16)
    for i in range(3):
        window[:, i * F : (i + 1) * F] = d_pre[(2 - i) * COL : (2 - i) * COL + EARLY]
    for t in range(3):
        rows = slice(t * 3 * C, (t + 1) * 3 * C)
        taps[rows] = matmul(features_t[rows, :EARLY], window[...])
    projs[...] = matmul(hidden_t[:, :HALF], d_out[...])


def back_second_kernel(
    core_ref, keep_ref, own, other, slope, proj, weights, features_t, hidden_t,
    d_pre_a, low_a, mid_a, high_a, taps, projs, low_out, mid, high, grads, d_pre, window, d_out, low, sem,
):
    d_pre[0 : 5 * COL] = d_pre_a[HALF - 4 * COL :]
    d_pre[5 * COL + HALF :] = jnp.zeros((COL, F), bf16)
    back_rows(core_ref, (own,), (other,), slope.at[HALF:], proj, d_pre, 5 * COL, d_out)
    low[:EARLY] = low_a[...]
    mid[:EARLY] = mid_a[...]
    high[:EARLY] = high_a[...]
    late = ROWS - EARLY
    for k in range(4):
        step = late // 4
        total = back_features(d_pre, weights, k * step, step)
        cells = slice(EARLY + k * step, EARLY + (k + 1) * step)
        low[cells] = total[:, :C].astype(bf16)
        mid[cells] = total[:, C : 2 * C]
        high[cells] = total[:, 2 * C :].astype(bf16)
    low_copy = pltpu.make_async_copy(low, low_out, sem)
    low_copy.start()
    for i in range(3):
        window[:, i * F : (i + 1) * F] = d_pre[(2 - i) * COL : (2 - i) * COL + late]
    off_centre = keep_ref[0]
    for t in range(3):
        rows = slice(t * 3 * C, (t + 1) * 3 * C)
        block = taps[rows] + matmul(features_t[rows, EARLY:], window[...])
        for i in range(3):
            for j in range(3):
                tap = (t * 9 + i * 3 + j) * C
                piece = block[j * C : (j + 1) * C, i * F : (i + 1) * F]
                if (t, i, j) != (1, 1, 1):
                    piece = piece * off_centre
                grads[tap : tap + C] = piece.astype(bf16)
    grads[TAPS:] = (projs[...] + matmul(hidden_t[:, HALF:], d_out[...])).astype(bf16)
    low_copy.wait()


def core_split_kernel(core_ref, low, mid, high, kept, sent, total):
    for q in range(4):
        cells = slice(q * QUART, (q + 1) * QUART)
        total[q] = mid[cells] + low[cells].astype(f32) + high[cells].astype(f32)
    core = core_ref[0]
    for row in range(2):
        kept[row] = total[2 * row + core]
        sent[row] = total[2 * row + 1 - core].astype(bf16)


def chip_split_kernel(row_ref, kept, recv, mine, sent):
    row = row_ref[0]
    mine[...] = kept[row] + recv[row].astype(f32)
    sent[...] = (kept[1 - row] + recv[1 - row].astype(f32)).astype(bf16)


def sum_of(parts):
    acc = parts[0].astype(f32)
    for k in range(1, parts.shape[0]):
        acc = acc + parts[k].astype(f32)
    return acc.astype(bf16)


def sum_kernel(parts, copies):
    total = sum_of(parts)
    for k in range(copies.shape[0]):
        copies[k] = total


def widen_kernel(total, taps_out, proj_out, wide, sems):
    moves = []
    for k in range(4):
        first = k * TAPS // 4
        last = first + TAPS // 4
        wide[first:last] = total[first:last].astype(f32)
        moves.append(pltpu.make_async_copy(wide.at[first:last], taps_out.at[first:last], sems.at[k]))
        moves[-1].start()
    wide[TAPS:] = total[TAPS:].astype(f32)
    moves.append(pltpu.make_async_copy(wide.at[TAPS:], proj_out, sems.at[4]))
    moves[-1].start()
    for move in moves:
        move.wait()


def call(kernel, outs, specs, scratch, flops, *args, place=VMEM):
    return pl.pallas_call(
        kernel,
        out_shape=[jax.ShapeDtypeStruct(*o) for o in outs],
        in_specs=specs,
        out_specs=place if isinstance(place, list) else [place] * len(outs),
        scratch_shapes=scratch,
        compiler_params=pltpu.CompilerParams(vmem_limit_bytes=12 * 1024 * 1024),
        cost_estimate=pl.CostEstimate(flops=flops, bytes_accessed=flops // 1000, transcendentals=0),
    )(*args)


def depth_pairs(mesh_gz, sign):
    strides = (0, 1, 2, 4)
    pairs = []
    for g in range(mesh_gz):
        for b in range(1, 4):
            target = g + sign * strides[b]
            if 0 <= target < mesh_gz:
                pairs.append((g * 4 + b, target * 4 + b))
    return pairs


def exchanged(parts, axis):
    return jnp.concatenate([lax.ppermute(part, axis, SWAP) for part in parts], axis=0).astype(f32)


def shards(slabs, features, tap_weights, branch_bias, proj_weights, out_bias, cotangent):
    branch = lax.axis_index(BR)
    core = lax.axis_index("c")
    row = lax.axis_index("yl")
    core_arg = core.astype(jnp.int32)[None]
    row_arg = row.astype(jnp.int32)[None]
    up = depth_pairs(slabs, 1)
    down = depth_pairs(slabs, -1)
    everywhere = GZ + BR
    proj = proj_weights[0]

    centre = lax.all_gather(features.reshape(QUART, C), BR, axis=0, tiled=True)
    tap = jnp.arange(27).reshape(3, 3, 3)
    off_centre = jnp.where(branch > 0, 1.0, 0.0).astype(f32)
    mask = jnp.where(tap == 13, 1.0, off_centre).astype(bf16)
    cot_mine = cotangent.reshape(QUART, F)
    centre, cot_mine = lax.optimization_barrier((centre, cot_mine))
    below = lax.ppermute(centre, everywhere, up)
    above = lax.ppermute(centre, everywhere, down)
    cot_pair = lax.ppermute(cot_mine, "yl", SWAP)
    masked = tap_weights[0] * mask[:, :, :, None, None]
    by_window = masked.transpose(0, 1, 3, 2, 4).reshape(3, 3 * C, 3 * F)
    weights_mid = by_window[1]
    weights_out = jnp.concatenate([by_window[0], by_window[2]], axis=0)
    weights_bwd = masked.transpose(2, 0, 3, 1, 4).reshape(9 * C, 3 * F)
    (base,) = call(
        centre_kernel,
        [((ROWS, F), f32)],
        [VMEM] * 3,
        [pltpu.VMEM((ROWS + 2 * COL, C), bf16)],
        2 * ROWS * 9 * C * F,
        centre, weights_mid, branch_bias,
    )
    below, above, cot_pair, base, weights_out, weights_bwd = lax.optimization_barrier(
        (below, above, cot_pair, base, weights_out, weights_bwd)
    )

    def forward_half(half, base):
        return call(
            functools.partial(forward_kernel, half),
            [((HALF, F), f32), ((HALF, F), bf16), ((QUART, F), f32)] + [((QUART // 2, F), bf16)] * 2,
            [SMEM] + [VMEM] * 5,
            [pltpu.VMEM((HALF + 2 * COL, C), bf16)] * 2 + [pltpu.VMEM((2, QUART, F), f32)],
            1000,
            core_arg, below, above, weights_out, base, proj,
        )

    preact_a, hidden_a, keep_a, *send_a = forward_half(0, base)
    chip_a = keep_a + exchanged(send_a, "c")
    preact_b, hidden_b, keep_b, *send_b = forward_half(1, base)
    chip_send_a, *send_b = lax.optimization_barrier((chip_a.astype(bf16), *send_b))
    recv_a = lax.ppermute(chip_send_a, "yl", SWAP)
    chip_b = keep_b + exchanged(send_b, "c")
    chip_send_b, preact_b = lax.optimization_barrier((chip_b.astype(bf16), preact_b))
    recv_b = lax.ppermute(chip_send_b, "yl", SWAP)
    slope, hidden_t, features_t = call(
        prepare_kernel,
        [((ROWS, F), f32), ((F, ROWS), bf16), ((9 * C, ROWS), bf16)],
        [VMEM] * 7,
        [],
        1000,
        below, centre, above, preact_a, preact_b, hidden_a, hidden_b,
    )
    recv_a, slope, hidden_t, features_t = lax.optimization_barrier((recv_a, slope, hidden_t, features_t))

    own_a = call(
        first_output_kernel,
        [((QUART // 2, F), bf16), ((QUART // 2, F), bf16)],
        [SMEM] + [VMEM] * 5,
        [],
        1000,
        row_arg, chip_a, recv_a, out_bias[None], cot_mine, cot_pair,
    )
    other_a = [lax.ppermute(part, "c", SWAP) for part in own_a]
    (head_a,) = call(
        first_head_kernel, [((QUART, F), bf16)], [VMEM] * 3, [], 1000, chip_a, recv_a, out_bias[None]
    )
    head_a, *other_a = lax.optimization_barrier((head_a, *other_a))
    d_pre_a, low_a, mid_a, high_a, taps_a, projs_a = call(
        back_first_kernel,
        [
            ((HALF + COL, F), bf16),
            ((EARLY, C), bf16),
            ((EARLY, C), f32),
            ((EARLY, C), bf16),
            ((9 * C, 3 * F), f32),
            ((F, F), f32),
        ],
        [SMEM] + [VMEM] * 9,
        [pltpu.VMEM((EARLY, 3 * F), bf16), pltpu.VMEM((HALF, F), bf16)],
        1000,
        core_arg, *own_a, *other_a, slope, proj, weights_bwd, features_t, hidden_t,
    )
    recv_b, taps_a, d_pre_a = lax.optimization_barrier((recv_b, taps_a, d_pre_a))
    (own_b,) = call(
        second_output_kernel,
        [((QUART, F), bf16)],
        [SMEM] + [VMEM] * 5,
        [],
        1000,
        row_arg, chip_b, recv_b, out_bias[None], cot_mine, cot_pair,
    )
    other_b = lax.ppermute(own_b, "c", SWAP)
    (head_out,) = call(
        second_head_kernel,
        [((QUART, F), bf16)],
        [SMEM] + [VMEM] * 4,
        [],
        1000,
        row_arg, chip_b, recv_b, out_bias[None], head_a,
    )
    head_out, other_b = lax.optimization_barrier((head_out, other_b))
    low, mid, high, grads = call(
        back_second_kernel,
        [((ROWS, C), bf16), ((ROWS, C), f32), ((ROWS, C), bf16), ((GRAD_ROWS, F), bf16)],
        [SMEM, SMEM] + [VMEM] * 13,
        [
            pltpu.VMEM((HALF + 6 * COL, F), bf16),
            pltpu.VMEM((ROWS - EARLY, 3 * F), bf16),
            pltpu.VMEM((HALF, F), bf16),
            pltpu.VMEM((ROWS, C), bf16),
            pltpu.SemaphoreType.DMA(()),
        ],
        2 * ROWS * 27 * C * F,
        core_arg, off_centre[None], own_b, other_b, slope, proj, weights_bwd, features_t, hidden_t,
        d_pre_a, low_a, mid_a, high_a, taps_a, projs_a,
        place=[HBM, VMEM, VMEM, VMEM],
    )
    near = math.prod(lax.axis_size(a) for a in NEAR)
    far = lax.axis_size(FAR)
    share = GRAD_ROWS // near
    grads, low, mid, high = lax.optimization_barrier((grads, low, mid, high))
    part = lax.all_to_all(grads.reshape(near, share, F), NEAR, 0, 0, tiled=True)
    part, low, mid, high = lax.optimization_barrier((part, low, mid, high))

    def sum_for(peers, parts):
        return call(
            sum_kernel,
            [((peers, share, F), bf16)],
            [VMEM],
            [],
            1_000_000,
            parts,
        )[0]

    part = sum_for(far, part)
    from_low = lax.ppermute(low, everywhere, down)
    from_high = lax.ppermute(high, everywhere, up)
    part = lax.all_to_all(part, FAR, 0, 0, tiled=True)
    part = sum_for(near, part)

    kept, sent = call(
        core_split_kernel,
        [((2, QUART, C), f32), ((2, QUART, C), bf16)],
        [SMEM] + [VMEM] * 3,
        [pltpu.VMEM((4, QUART, C), f32)],
        1_000_000,
        core_arg, from_low, mid, from_high,
    )
    mine, sent = call(
        chip_split_kernel,
        [((QUART, C), f32), ((QUART, C), bf16)],
        [SMEM] + [VMEM] * 2,
        [],
        1_000_000,
        row_arg, kept, lax.ppermute(sent, "c", SWAP),
    )
    recv = lax.ppermute(sent, "yl", SWAP)
    feature_grad = (mine + recv.astype(f32)).astype(bf16)
    part, feature_grad = lax.optimization_barrier((part, feature_grad))
    total = lax.all_to_all(part, NEAR, 0, 0, tiled=True).reshape(GRAD_ROWS, F)
    taps, proj_total = call(
        widen_kernel,
        [((TAPS, F), f32), ((F, F), f32)],
        [VMEM],
        [pltpu.VMEM((GRAD_ROWS, F), f32), pltpu.SemaphoreType.DMA((5,))],
        1_000_000,
        total,
        place=HBM,
    )
    return (
        head_out.reshape(cotangent.shape),
        feature_grad.reshape(features.shape),
        taps.reshape(1, 3, 3, 3, C, F),
        proj_total.reshape(1, F, F),
    )


def solution(mesh):
    slabs = mesh.shape["gz"]
    split = (4, 2, 4, 2) if slabs == 64 else (slabs, 1, 1, 1)
    fine = Mesh(mesh.devices.reshape(split + (2, 2)), GZ + BR)
    in_specs = (
        P(BR, GZ, None, None),
        P(BR, None, None, None, None, None),
        P(BR, None),
        P(BR, None, None),
        P(),
        P(BR, GZ, None, None),
    )
    out_specs = (
        P(BR, GZ, None, None),
        P(BR, GZ, None, None),
        P(BR, None, None, None, None, None),
        P(BR, None, None),
    )
    return jax.shard_map(
        functools.partial(shards, slabs), mesh=fine, in_specs=in_specs, out_specs=out_specs, check_vma=False
    )
```

```python
import functools
import math

import jax
import jax.numpy as jnp
from jax import lax
from jax.experimental import pallas as pl
from jax.experimental.pallas import tpu as pltpu
from jax.sharding import Mesh
from jax.sharding import PartitionSpec as P

C = 128
F = 256
COL = 64
ROWS = 2048
HALF = 1024
EARLY = 12 * COL
QUART = 512
TAPS = 27 * C
GRAD_ROWS = TAPS + F
bf16 = jnp.bfloat16
f32 = jnp.float32
GZ = ("zh", "zl", "x", "yh")
NEAR = ("zl", "x", "yh")
FAR = "zh"
BR = ("yl", "c")
SWAP = [(0, 1), (1, 0)]
VMEM = pl.BlockSpec(memory_space=pltpu.VMEM)
HBM = pl.BlockSpec(memory_space=pltpu.HBM)
SMEM = pl.BlockSpec(memory_space=pltpu.SMEM)


def silu_slope(values):
    logistic = jax.nn.sigmoid(values)
    return logistic * (1.0 + values * (1.0 - logistic))


def height_of(rows, lanes):
    return lax.broadcasted_iota(jnp.int32, (rows, lanes), 0) & 15


def from_below(values):
    rolled = pltpu.roll(values, 1, 0)
    return jnp.where(height_of(*values.shape) == 0, 0.0, rolled)


def from_above(values):
    rolled = pltpu.roll(values, values.shape[0] - 1, 0)
    return jnp.where(height_of(*values.shape) == 15, 0.0, rolled)


def matmul(lhs, rhs):
    return jnp.dot(lhs, rhs, preferred_element_type=f32)


def matmul_rt(lhs, rhs):
    return lax.dot_general(lhs, rhs, (((1,), (1,)), ((), ())), preferred_element_type=f32)


def pad_columns(padded, slab):
    padded[0:COL] = jnp.zeros((COL, C), bf16)
    padded[COL + ROWS : 2 * COL + ROWS] = jnp.zeros((COL, C), bf16)
    padded[COL : COL + ROWS] = slab[...]


def pad_half(padded, slab, half):
    if half == 0:
        padded[0:COL] = jnp.zeros((COL, C), bf16)
        padded[COL:] = slab[0 : HALF + COL]
    else:
        padded[0 : HALF + COL] = slab[HALF - COL :]
        padded[HALF + COL :] = jnp.zeros((COL, C), bf16)


def over_height(parts):
    return parts[:, F : 2 * F] + from_below(parts[:, :F]) + from_above(parts[:, 2 * F :])


def centre_kernel(centre, weights, bias, base, padded):
    pad_columns(padded, centre)
    for q in range(4):
        start = q * QUART
        window = jnp.concatenate([padded[start + i * COL : start + i * COL + QUART] for i in range(3)], axis=1)
        base[start : start + QUART] = bias[...] + over_height(matmul(window, weights[...]))


def forward_kernel(
    half, core_ref, below, above, weights, base, proj, preact, hidden, keep, send_0, send_1, low, high, sides
):
    pad_half(low, below, half)
    pad_half(high, above, half)
    for side in range(2):
        start = side * QUART
        cells = slice(start, start + QUART)
        window = jnp.concatenate(
            [slab[start + i * COL : start + i * COL + QUART] for slab in (low, high) for i in range(3)], axis=1
        )
        value = base[half * HALF + start : half * HALF + start + QUART] + over_height(matmul(window, weights[...]))
        preact[cells] = value
        active = (value * jax.nn.sigmoid(value)).astype(bf16)
        hidden[cells] = active
        sides[side] = matmul(active, proj[...])
    core = core_ref[0]
    keep[...] = sides[core]
    send_0[...] = sides[1 - core, : QUART // 2].astype(bf16)
    send_1[...] = sides[1 - core, QUART // 2 :].astype(bf16)


def prepare_kernel(
    below, centre, above, preact_a, preact_b, hidden_a, hidden_b, slope, hidden_t, features_t
):
    for q in range(4):
        cells = slice(q * QUART, (q + 1) * QUART)
        local = slice(q % 2 * QUART, (q % 2 + 1) * QUART)
        preact, hidden = ((preact_a, hidden_a), (preact_b, hidden_b))[q // 2]
        slope[cells] = silu_slope(preact[local])
        hidden_t[:, cells] = hidden[local].astype(f32).T.astype(bf16)
        for t, slab in enumerate((below, centre, above)):
            value = slab[cells].astype(f32)
            for j, moved in enumerate((from_below(value), value, from_above(value))):
                block = (t * 3 + j) * C
                features_t[block : block + C, cells] = moved.T.astype(bf16)


def d_out_of(summed, cot):
    return (cot.astype(f32) * silu_slope(summed)).astype(bf16)


def head_of(summed):
    return (summed * jax.nn.sigmoid(summed)).astype(bf16)


def first_output_kernel(row_ref, chip_sum, recv, bias, cot_mine, cot_pair, own_0, own_1):
    for k, own in enumerate((own_0, own_1)):
        cells = slice(k * (QUART // 2), (k + 1) * (QUART // 2))
        summed = chip_sum[cells] + recv[cells].astype(f32) + bias[...]
        own[...] = d_out_of(summed, jnp.where(row_ref[0] == 0, cot_mine[cells], cot_pair[cells]))


def second_output_kernel(row_ref, chip_sum, recv, bias, cot_mine, cot_pair, own):
    summed = chip_sum[...] + recv[...].astype(f32) + bias[...]
    own[...] = d_out_of(summed, jnp.where(row_ref[0] == 1, cot_mine[...], cot_pair[...]))


def first_head_kernel(chip_sum, recv, bias, head):
    head[...] = head_of(chip_sum[...] + recv[...].astype(f32) + bias[...])


def second_head_kernel(row_ref, chip_sum, recv, bias, head_a, head):
    summed = chip_sum[...] + recv[...].astype(f32) + bias[...]
    head[...] = jnp.where(row_ref[0] == 0, head_a[...], head_of(summed))


def height_sum(parts):
    return parts[:, 3 * C : 6 * C] + from_above(parts[:, : 3 * C]) + from_below(parts[:, 6 * C :])


def back_rows(core_ref, own, other, slope, proj, d_pre, at, d_out):
    for side in range(2):
        start = side * QUART
        for mine, theirs in zip(own, other):
            count = mine.shape[0]
            rows = jnp.where(core_ref[0] == side, mine[...], theirs[...])
            d_out[start : start + count] = rows
            d_hidden = matmul_rt(rows, proj[...])
            d_pre[at + start : at + start + count] = (d_hidden * slope[start : start + count]).astype(bf16)
            start += count


def back_features(d_pre, weights, start, count):
    window = jnp.concatenate(
        [d_pre[start + (2 - i) * COL : start + (2 - i) * COL + count] for i in range(3)], axis=1
    )
    return height_sum(matmul_rt(window, weights[...]))


def back_first_kernel(
    core_ref, own_0, own_1, other_0, other_1, slope, proj, weights, features_t, hidden_t,
    d_pre, low, mid, high, taps, projs, window, d_out,
):
    d_pre[0:COL] = jnp.zeros((COL, F), bf16)
    back_rows(core_ref, (own_0, own_1), (other_0, other_1), slope, proj, d_pre, COL, d_out)
    for k in range(2):
        step = EARLY // 2
        total = back_features(d_pre, weights, k * step, step)
        cells = slice(k * step, (k + 1) * step)
        low[cells] = total[:, :C].astype(bf16)
        mid[cells] = total[:, C : 2 * C]
        high[cells] = total[:, 2 * C :].astype(bf16)
    for i in range(3):
        window[:, i * F : (i + 1) * F] = d_pre[(2 - i) * COL : (2 - i) * COL + EARLY]
    for t in range(3):
        rows = slice(t * 3 * C, (t + 1) * 3 * C)
        taps[rows] = matmul(features_t[rows, :EARLY], window[...])
    projs[...] = matmul(hidden_t[:, :HALF], d_out[...])


def back_second_kernel(
    core_ref, keep_ref, own, other, slope, proj, weights, features_t, hidden_t,
    d_pre_a, low_a, mid_a, high_a, taps, projs, low_out, mid, high, grads, d_pre, window, d_out, low, sem,
):
    d_pre[0 : 5 * COL] = d_pre_a[HALF - 4 * COL :]
    d_pre[5 * COL + HALF :] = jnp.zeros((COL, F), bf16)
    back_rows(core_ref, (own,), (other,), slope.at[HALF:], proj, d_pre, 5 * COL, d_out)
    low[:EARLY] = low_a[...]
    mid[:EARLY] = mid_a[...]
    high[:EARLY] = high_a[...]
    late = ROWS - EARLY
    for k in range(4):
        step = late // 4
        total = back_features(d_pre, weights, k * step, step)
        cells = slice(EARLY + k * step, EARLY + (k + 1) * step)
        low[cells] = total[:, :C].astype(bf16)
        mid[cells] = total[:, C : 2 * C]
        high[cells] = total[:, 2 * C :].astype(bf16)
    low_copy = pltpu.make_async_copy(low, low_out, sem)
    low_copy.start()
    for i in range(3):
        window[:, i * F : (i + 1) * F] = d_pre[(2 - i) * COL : (2 - i) * COL + late]
    off_centre = keep_ref[0]
    for t in range(3):
        rows = slice(t * 3 * C, (t + 1) * 3 * C)
        block = taps[rows] + matmul(features_t[rows, EARLY:], window[...])
        for i in range(3):
            for j in range(3):
                tap = (t * 9 + i * 3 + j) * C
                piece = block[j * C : (j + 1) * C, i * F : (i + 1) * F]
                if (t, i, j) != (1, 1, 1):
                    piece = piece * off_centre
                grads[tap : tap + C] = piece.astype(bf16)
    grads[TAPS:] = (projs[...] + matmul(hidden_t[:, HALF:], d_out[...])).astype(bf16)
    low_copy.wait()


def core_split_kernel(core_ref, low, mid, high, kept, sent, total):
    for q in range(4):
        cells = slice(q * QUART, (q + 1) * QUART)
        total[q] = mid[cells] + low[cells].astype(f32) + high[cells].astype(f32)
    core = core_ref[0]
    for row in range(2):
        kept[row] = total[2 * row + core]
        sent[row] = total[2 * row + 1 - core].astype(bf16)


def chip_split_kernel(row_ref, kept, recv, mine, sent):
    row = row_ref[0]
    mine[...] = kept[row] + recv[row].astype(f32)
    sent[...] = (kept[1 - row] + recv[1 - row].astype(f32)).astype(bf16)


def sum_of(parts):
    acc = parts[0].astype(f32)
    for k in range(1, parts.shape[0]):
        acc = acc + parts[k].astype(f32)
    return acc.astype(bf16)


def sum_kernel(parts, copies):
    total = sum_of(parts)
    for k in range(copies.shape[0]):
        copies[k] = total


def widen_kernel(total, taps_out, proj_out, wide, sems):
    moves = []
    for k in range(8):
        first = k * TAPS // 8
        last = first + TAPS // 8
        wide[first:last] = total[first:last].astype(f32)
        moves.append(pltpu.make_async_copy(wide.at[first:last], taps_out.at[first:last], sems.at[k]))
        moves[-1].start()
    wide[TAPS:] = total[TAPS:].astype(f32)
    moves.append(pltpu.make_async_copy(wide.at[TAPS:], proj_out, sems.at[8]))
    moves[-1].start()
    for move in moves:
        move.wait()


def call(kernel, outs, specs, scratch, flops, *args, place=VMEM):
    return pl.pallas_call(
        kernel,
        out_shape=[jax.ShapeDtypeStruct(*o) for o in outs],
        in_specs=specs,
        out_specs=place if isinstance(place, list) else [place] * len(outs),
        scratch_shapes=scratch,
        compiler_params=pltpu.CompilerParams(vmem_limit_bytes=12 * 1024 * 1024),
        cost_estimate=pl.CostEstimate(flops=flops, bytes_accessed=flops // 1000, transcendentals=0),
    )(*args)


def depth_pairs(mesh_gz, sign):
    strides = (0, 1, 2, 4)
    pairs = []
    for g in range(mesh_gz):
        for b in range(1, 4):
            target = g + sign * strides[b]
            if 0 <= target < mesh_gz:
                pairs.append((g * 4 + b, target * 4 + b))
    return pairs


def exchanged(parts, axis):
    return jnp.concatenate([lax.ppermute(part, axis, SWAP) for part in parts], axis=0).astype(f32)


def shards(slabs, features, tap_weights, branch_bias, proj_weights, out_bias, cotangent):
    branch = lax.axis_index(BR)
    core = lax.axis_index("c")
    row = lax.axis_index("yl")
    core_arg = core.astype(jnp.int32)[None]
    row_arg = row.astype(jnp.int32)[None]
    up = depth_pairs(slabs, 1)
    down = depth_pairs(slabs, -1)
    everywhere = GZ + BR
    proj = proj_weights[0]

    centre = lax.all_gather(features.reshape(QUART, C), BR, axis=0, tiled=True)
    tap = jnp.arange(27).reshape(3, 3, 3)
    off_centre = jnp.where(branch > 0, 1.0, 0.0).astype(f32)
    mask = jnp.where(tap == 13, 1.0, off_centre).astype(bf16)
    cot_mine = cotangent.reshape(QUART, F)
    centre, cot_mine = lax.optimization_barrier((centre, cot_mine))
    below = lax.ppermute(centre, everywhere, up)
    above = lax.ppermute(centre, everywhere, down)
    cot_pair = lax.ppermute(cot_mine, "yl", SWAP)
    masked = tap_weights[0] * mask[:, :, :, None, None]
    by_window = masked.transpose(0, 1, 3, 2, 4).reshape(3, 3 * C, 3 * F)
    weights_mid = by_window[1]
    weights_out = jnp.concatenate([by_window[0], by_window[2]], axis=0)
    weights_bwd = masked.transpose(2, 0, 3, 1, 4).reshape(9 * C, 3 * F)
    (base,) = call(
        centre_kernel,
        [((ROWS, F), f32)],
        [VMEM] * 3,
        [pltpu.VMEM((ROWS + 2 * COL, C), bf16)],
        2 * ROWS * 9 * C * F,
        centre, weights_mid, branch_bias,
    )
    below, above, cot_pair, base, weights_out, weights_bwd = lax.optimization_barrier(
        (below, above, cot_pair, base, weights_out, weights_bwd)
    )

    def forward_half(half, base):
        return call(
            functools.partial(forward_kernel, half),
            [((HALF, F), f32), ((HALF, F), bf16), ((QUART, F), f32)] + [((QUART // 2, F), bf16)] * 2,
            [SMEM] + [VMEM] * 5,
            [pltpu.VMEM((HALF + 2 * COL, C), bf16)] * 2 + [pltpu.VMEM((2, QUART, F), f32)],
            1000,
            core_arg, below, above, weights_out, base, proj,
        )

    preact_a, hidden_a, keep_a, *send_a = forward_half(0, base)
    chip_a = keep_a + exchanged(send_a, "c")
    preact_b, hidden_b, keep_b, *send_b = forward_half(1, base)
    chip_send_a, *send_b = lax.optimization_barrier((chip_a.astype(bf16), *send_b))
    recv_a = lax.ppermute(chip_send_a, "yl", SWAP)
    chip_b = keep_b + exchanged(send_b, "c")
    chip_send_b, preact_b = lax.optimization_barrier((chip_b.astype(bf16), preact_b))
    recv_b = lax.ppermute(chip_send_b, "yl", SWAP)
    slope, hidden_t, features_t = call(
        prepare_kernel,
        [((ROWS, F), f32), ((F, ROWS), bf16), ((9 * C, ROWS), bf16)],
        [VMEM] * 7,
        [],
        1000,
        below, centre, above, preact_a, preact_b, hidden_a, hidden_b,
    )
    recv_a, slope, hidden_t, features_t = lax.optimization_barrier((recv_a, slope, hidden_t, features_t))

    own_a = call(
        first_output_kernel,
        [((QUART // 2, F), bf16), ((QUART // 2, F), bf16)],
        [SMEM] + [VMEM] * 5,
        [],
        1000,
        row_arg, chip_a, recv_a, out_bias[None], cot_mine, cot_pair,
    )
    other_a = [lax.ppermute(part, "c", SWAP) for part in own_a]
    (head_a,) = call(
        first_head_kernel, [((QUART, F), bf16)], [VMEM] * 3, [], 1000, chip_a, recv_a, out_bias[None]
    )
    head_a, *other_a = lax.optimization_barrier((head_a, *other_a))
    d_pre_a, low_a, mid_a, high_a, taps_a, projs_a = call(
        back_first_kernel,
        [
            ((HALF + COL, F), bf16),
            ((EARLY, C), bf16),
            ((EARLY, C), f32),
            ((EARLY, C), bf16),
            ((9 * C, 3 * F), f32),
            ((F, F), f32),
        ],
        [SMEM] + [VMEM] * 9,
        [pltpu.VMEM((EARLY, 3 * F), bf16), pltpu.VMEM((HALF, F), bf16)],
        1000,
        core_arg, *own_a, *other_a, slope, proj, weights_bwd, features_t, hidden_t,
    )
    recv_b, taps_a, d_pre_a = lax.optimization_barrier((recv_b, taps_a, d_pre_a))
    (own_b,) = call(
        second_output_kernel,
        [((QUART, F), bf16)],
        [SMEM] + [VMEM] * 5,
        [],
        1000,
        row_arg, chip_b, recv_b, out_bias[None], cot_mine, cot_pair,
    )
    other_b = lax.ppermute(own_b, "c", SWAP)
    (head_out,) = call(
        second_head_kernel,
        [((QUART, F), bf16)],
        [SMEM] + [VMEM] * 4,
        [],
        1000,
        row_arg, chip_b, recv_b, out_bias[None], head_a,
    )
    head_out, other_b = lax.optimization_barrier((head_out, other_b))
    low, mid, high, grads = call(
        back_second_kernel,
        [((ROWS, C), bf16), ((ROWS, C), f32), ((ROWS, C), bf16), ((GRAD_ROWS, F), bf16)],
        [SMEM, SMEM] + [VMEM] * 13,
        [
            pltpu.VMEM((HALF + 6 * COL, F), bf16),
            pltpu.VMEM((ROWS - EARLY, 3 * F), bf16),
            pltpu.VMEM((HALF, F), bf16),
            pltpu.VMEM((ROWS, C), bf16),
            pltpu.SemaphoreType.DMA(()),
        ],
        2 * ROWS * 27 * C * F,
        core_arg, off_centre[None], own_b, other_b, slope, proj, weights_bwd, features_t, hidden_t,
        d_pre_a, low_a, mid_a, high_a, taps_a, projs_a,
        place=[HBM, VMEM, VMEM, VMEM],
    )
    near = math.prod(lax.axis_size(a) for a in NEAR)
    far = lax.axis_size(FAR)
    share = GRAD_ROWS // near
    grads, low, mid, high = lax.optimization_barrier((grads, low, mid, high))
    part = lax.all_to_all(grads.reshape(near, share, F), NEAR, 0, 0, tiled=True)
    part, low, mid, high = lax.optimization_barrier((part, low, mid, high))

    def sum_for(peers, parts):
        return call(
            sum_kernel,
            [((peers, share, F), bf16)],
            [VMEM],
            [],
            1_000_000,
            parts,
        )[0]

    part = sum_for(far, part)
    from_low = lax.ppermute(low, everywhere, down)
    from_high = lax.ppermute(high, everywhere, up)
    part = lax.all_to_all(part, FAR, 0, 0, tiled=True)
    part = sum_for(near, part)

    kept, sent = call(
        core_split_kernel,
        [((2, QUART, C), f32), ((2, QUART, C), bf16)],
        [SMEM] + [VMEM] * 3,
        [pltpu.VMEM((4, QUART, C), f32)],
        1_000_000,
        core_arg, from_low, mid, from_high,
    )
    mine, sent = call(
        chip_split_kernel,
        [((QUART, C), f32), ((QUART, C), bf16)],
        [SMEM] + [VMEM] * 2,
        [],
        1_000_000,
        row_arg, kept, lax.ppermute(sent, "c", SWAP),
    )
    recv = lax.ppermute(sent, "yl", SWAP)
    feature_grad = (mine + recv.astype(f32)).astype(bf16)
    part, feature_grad = lax.optimization_barrier((part, feature_grad))
    total = lax.all_to_all(part, NEAR, 0, 0, tiled=True).reshape(GRAD_ROWS, F)
    taps, proj_total = call(
        widen_kernel,
        [((TAPS, F), f32), ((F, F), f32)],
        [VMEM],
        [pltpu.VMEM((GRAD_ROWS, F), f32), pltpu.SemaphoreType.DMA((9,))],
        1_000_000,
        total,
        place=HBM,
    )
    return (
        head_out.reshape(cotangent.shape),
        feature_grad.reshape(features.shape),
        taps.reshape(1, 3, 3, 3, C, F),
        proj_total.reshape(1, F, F),
    )


def solution(mesh):
    slabs = mesh.shape["gz"]
    split = (4, 2, 4, 2) if slabs == 64 else (slabs, 1, 1, 1)
    fine = Mesh(mesh.devices.reshape(split + (2, 2)), GZ + BR)
    in_specs = (
        P(BR, GZ, None, None),
        P(BR, None, None, None, None, None),
        P(BR, None),
        P(BR, None, None),
        P(),
        P(BR, GZ, None, None),
    )
    out_specs = (
        P(BR, GZ, None, None),
        P(BR, GZ, None, None),
        P(BR, None, None, None, None, None),
        P(BR, None, None),
    )
    return jax.shard_map(
        functools.partial(shards, slabs), mesh=fine, in_specs=in_specs, out_specs=out_specs, check_vma=False
    )
```
